128 devices in a mesh: row: 8 (over x, y_hi), col: 16 (over z, y_lo, core).
Axes of the slice: x: 4, y: 4 (y_hi: 2, y_lo: 2; y = y_hi * 2 + y_lo), z: 4, core: 2. Of those that a mesh axis runs over, the one named last changes fastest.
Arguments:
- moment_x: bfloat16 [128, 512, 512], P('row', 'col'), may hold values from -0.25 to 0.25
- moment_s: bfloat16 [128, 512, 512], P('row', 'col'), may hold values from -0.25 to 0.25
- coeffs: bfloat16 [128, 32, 512, 512], P(('row', 'col')), may hold values from -0.125 to 0.125
- slot_con: int32 [128, 32], replicated, may hold values from 0 to 8191, as said below
- con_pos: int32 [8192], replicated, may hold values from 0 to 8191, as said below
- schur_prev: float32 [8192, 8192], P('row', 'col'), may hold values from -6 to 6
- panel_inv: float32 [256, 256], replicated, as said below
Outputs:
- updated: float32 [8192, 8192], P('row', 'col')
- panel_factor: float32 [8192, 256], P('row')
The draws below stay inside these ranges and needn't reach their ends.
Inputs may be any that keep to these rules, and one draw needn't show every extreme that they name: Within each block the 32 slots name distinct constraints; with positions = con_pos[slot_con], slot s of every block has positions // 512 == s // 2. `con_pos`: A permutation of the 8192 constraints. `panel_inv`: upper triangular with a positive diagonal.
All inputs are finite; a program needn't handle non-finite values.
Results may differ from the reference program's by a relative error of at most 0.0003.
Values may be sent and summed in bfloat16 or wider, within the bound.
A program may use at most 192 MiB of HBM per device.

```python
import jax
import jax.numpy as jnp
from jax import lax

BLOCK_ORDER = 512
SLOTS_PER_BLOCK = 32
TILE = 16
PW = 256
BLOCK_COUNT = 128
NCON = 8192
COLUMNS_PER_PART = 512
SLOTS_PER_SHARD = 2
N_COL = 16


def layout_tables(key):
    key_perm = jax.random.fold_in(key, 11)
    key_offset = jax.random.fold_in(key, 12)
    shard_total = SLOTS_PER_BLOCK // SLOTS_PER_SHARD
    con_table = jax.random.permutation(key_perm, NCON).astype(jnp.int32)
    keys = jax.random.split(key_offset, BLOCK_COUNT * shard_total)
    start_offsets = jax.vmap(lambda single: jax.random.permutation(single, COLUMNS_PER_PART)[:SLOTS_PER_SHARD])(keys).astype(jnp.int32)
    first_pos = con_table[0]
    last_pos = con_table[NCON - 1]
    group_first = first_pos // COLUMNS_PER_PART
    group_last = shard_total + last_pos // COLUMNS_PER_PART
    group_ids = jnp.arange(BLOCK_COUNT * shard_total, dtype=jnp.int32)
    shift = jnp.where(group_ids == group_first, first_pos % COLUMNS_PER_PART - start_offsets[:, 0], jnp.where(group_ids == group_last, last_pos % COLUMNS_PER_PART - start_offsets[:, 0], 0))
    start_offsets = (start_offsets + shift[:, None]) % COLUMNS_PER_PART
    slot_kinds = group_ids % shard_total
    stored_entries = (slot_kinds[:, None] * COLUMNS_PER_PART + start_offsets).reshape(BLOCK_COUNT, SLOTS_PER_BLOCK)
    inverse_table = jnp.zeros((NCON,), jnp.int32).at[con_table].set(jnp.arange(NCON, dtype=jnp.int32))
    return (inverse_table[stored_entries], con_table)


def draw_slot_con(key, part):
    return layout_tables(key)[0]


def draw_con_pos(key, part):
    return layout_tables(key)[1]


def draw_panel_inv(key, part):
    key_diag = jax.random.fold_in(key, 21)
    key_upper = jax.random.fold_in(key, 22)
    diagonal = jnp.exp(jax.random.uniform(key_diag, (PW,), jnp.float32, jnp.log(0.02), jnp.log(0.08)))
    upper = jax.random.normal(key_upper, (PW, PW), jnp.float32) * 0.015
    return jnp.triu(upper, 1) + jnp.diag(diagonal)


def levels(own_key, extent, pieces, least, high):
    loudness, own = 1.0, jax.random.fold_in(own_key, 6)
    for axis_at, blocks in pieces:
        steps = jnp.exp(jax.random.uniform(jax.random.fold_in(own, axis_at), (blocks,), jnp.float32, least / len(pieces), high / len(pieces)))
        loudness = loudness * jnp.repeat(steps, extent[axis_at] // blocks).reshape([-1 if axis == axis_at else 1 for axis in range(len(extent))])
    return loudness


def scatter_about(own_key, extent, width, most, shards=(), kind=jnp.bfloat16):
    result = jax.random.normal(own_key, extent, jnp.float32) * width
    if len(shards) > 0:
        result = levels(own_key, extent, shards, -0.22, 0.18) * result
    return jnp.clip(result, min=-most, max=most).astype(kind)


def setup_inputs(seed: int = 0) -> dict:
    streams_of = jax.random.split(jax.random.key(seed), 8)
    moment_x = scatter_about(streams_of[0], (BLOCK_COUNT, BLOCK_ORDER, BLOCK_ORDER), BLOCK_ORDER ** -0.5, 0.25, ((0, 8), (1, 16)))
    moment_s = scatter_about(streams_of[1], (BLOCK_COUNT, BLOCK_ORDER, BLOCK_ORDER), BLOCK_ORDER ** -0.5, 0.25, ((0, 8), (1, 16)))
    coeffs = scatter_about(streams_of[2], (BLOCK_COUNT, SLOTS_PER_BLOCK, BLOCK_ORDER, BLOCK_ORDER), (4 * BLOCK_ORDER) ** -0.5, 0.125, ((0, 128),))
    slot_con = draw_slot_con(jax.random.fold_in(streams_of[7], 71), 0)
    con_pos = draw_con_pos(jax.random.fold_in(streams_of[7], 71), 0)
    schur_prev = scatter_about(streams_of[5], (NCON, NCON), 1.0, 6.0, ((0, 8), (1, 16)), jnp.float32)
    panel_inv = draw_panel_inv(jax.random.fold_in(streams_of[7], 71), 0)
    return dict(moment_x=moment_x, moment_s=moment_s, coeffs=coeffs, slot_con=slot_con, con_pos=con_pos, schur_prev=schur_prev, panel_inv=panel_inv)


def reference(moment_x, moment_s, coeffs, slot_con, con_pos, schur_prev, panel_inv):
    positions = jnp.take(con_pos, slot_con, axis=0).astype(jnp.int32)

    def one_block(items):
        primal, inverse_dual, constraint_slots = items
        left = jnp.einsum("pq,nqr->npr", primal.astype(jnp.float32), constraint_slots.astype(jnp.float32)).astype(jnp.bfloat16)
        mapped_image = jnp.einsum("npr,rs->nps", left.astype(jnp.float32), inverse_dual.astype(jnp.float32)).astype(jnp.bfloat16)
        return jnp.dot(constraint_slots.reshape(SLOTS_PER_BLOCK, BLOCK_ORDER * BLOCK_ORDER), mapped_image.reshape(SLOTS_PER_BLOCK, BLOCK_ORDER * BLOCK_ORDER).T, preferred_element_type=jnp.float32)

    entries = lax.map(one_block, (moment_x, moment_s, coeffs))
    schur = schur_prev.at[positions[:, :, None], positions[:, None, :]].add(entries)
    factor_order = jnp.arange(PW, dtype=jnp.int32)
    stored_entries = ((factor_order % (TILE * N_COL)) // TILE) * COLUMNS_PER_PART + (factor_order // (TILE * N_COL)) * TILE + factor_order % TILE
    panel_factor = jnp.dot(schur[:, stored_entries], panel_inv, precision=lax.Precision.HIGHEST)
    updated = schur - jnp.dot(panel_factor, panel_factor.T, precision=lax.Precision.HIGHEST)
    return updated, panel_factor
```

```python
import functools

import jax
import jax.numpy as jnp
from jax import lax
from jax.experimental import pallas as pl
from jax.experimental.pallas import tpu as pltpu
from jax.sharding import PartitionSpec as P

TILE = 16
PW = 256
PART = 512
MESH = pl.DeviceIdType.MESH
F32 = jnp.float32
BF16 = jnp.bfloat16
PRIMAL, DUAL, SLAB, PART_ROWS, ENTRIES, SLAB_ENTRIES, PART_ENTRIES = range(7)


def dot(a, b, dims=((1,), (0,)), precision=None):
    return lax.dot_general(a, b, (dims, ((), ())), precision=precision, preferred_element_type=F32)


def iota(shape, axis):
    return lax.broadcasted_iota(jnp.int32, shape, axis)


def halves(value):
    high = value.astype(BF16)
    return high, (value - high.astype(F32)).astype(BF16)


def dot_halves(a, b, dims=((1,), (0,))):
    a_high, a_low = a
    b_high, b_low = b
    return dot(a_high, b_high, dims) + dot(a_high, b_low, dims) + dot(a_low, b_high, dims)


def flag(condition):
    return jnp.where(condition, 1.0, 0.0).astype(BF16)


def assemble_kernel(
    n_row, n_col,
    moment_x, moment_s, coeffs, slot_con, con_pos, schur_prev,
    slab_panel, part_panel, slab_entries, part_entries, local_pos,
    a_v, left_v, x_v, s_v, wide_v, own_panel, total, entry_v, gathered, chosen,
    a_sem, own_sem, send_sem, recv_sem,
):
    row = lax.axis_index("row")
    col = lax.axis_index("col")
    count, order = a_v.shape[0], a_v.shape[1]
    chunk = order // n_col
    home = lax.div(col, n_col // n_row)

    a_parts = a_sem.shape[0]
    per_part = count // a_parts

    def a_copy(part):
        where = pl.ds(part * per_part, per_part)
        return pltpu.make_async_copy(coeffs.at[0, where], a_v.at[where], a_sem.at[part])

    my_chunk = pl.ds(pl.multiple_of(col * chunk, chunk), chunk)
    my_tile = pl.ds(pl.multiple_of(col * TILE, TILE), TILE)
    wide_copy = pltpu.make_async_copy(schur_prev.at[:, pl.ds(0, wide_v.shape[1])], wide_v, own_sem.at[4])
    own_x = pltpu.make_async_copy(moment_x.at[col], x_v.at[my_chunk], own_sem.at[PRIMAL])
    own_s = pltpu.make_async_copy(moment_s.at[col], s_v.at[my_chunk], own_sem.at[DUAL])
    wide_copy.start()
    own_x.start()
    own_s.start()
    lax.fori_loop(0, a_parts, lambda part, _: a_copy(part).start(), None)

    barrier = pltpu.get_barrier_semaphore()

    def greet(r, c):
        pl.semaphore_signal(barrier, inc=1, device_id=(r, c), device_id_type=MESH)

    lax.fori_loop(1, n_col, lambda k, _: greet(row, lax.rem(col + k, n_col)), None)
    lax.fori_loop(1, n_row, lambda k, _: greet(lax.rem(row + k, n_row), col), None)

    def greet_home(j, _):
        @pl.when(jnp.logical_or(home != row, j != col))
        def _():
            greet(home, j)

    lax.fori_loop(0, n_col, greet_home, None)
    at_home = home == row
    pl.semaphore_wait(barrier, n_col - 1 + n_row - 1 + n_col - at_home.astype(jnp.int32))

    def send(src, dst, which, r, c):
        pltpu.make_async_remote_copy(
            src_ref=src, dst_ref=dst, send_sem=send_sem.at[which], recv_sem=recv_sem.at[which],
            device_id=(r, c), device_id_type=MESH,
        ).start()

    def to_col(which, src, dst):
        def step(k, _):
            peer = lax.rem(col + k, n_col)
            send(src(peer), dst, which, row, peer)
        lax.fori_loop(1, n_col, step, None)

    halves_here = n_col // n_row

    def to_parts(which, src, dst):
        def step(k, _):
            r = lax.rem(row + k, n_row)
            for half in range(halves_here):
                c = row * halves_here + half

                @pl.when(jnp.logical_or(r != row, c != col))
                def _():
                    send(src(half), dst, which, r, c)

                @pl.when(jnp.logical_and(r == row, c == col))
                def _():
                    pltpu.make_async_copy(src(half), dst, recv_sem.at[which]).start()
        lax.fori_loop(0, n_row, step, None)

    def wait_bytes(ref, sem):
        pltpu.make_async_copy(ref, ref, sem).wait()

    def wait_parts_sent(which, whole, less):
        @pl.when(at_home)
        def _():
            wait_bytes(less, send_sem.at[which])

        @pl.when(jnp.logical_not(at_home))
        def _():
            wait_bytes(whole, send_sem.at[which])

    to_col(PRIMAL, lambda peer: moment_x.at[peer], x_v.at[my_chunk])
    to_col(DUAL, lambda peer: moment_s.at[peer], s_v.at[my_chunk])

    blocks = slot_con.shape[0]
    con = slot_con[...]
    perm = flag(iota((blocks, blocks), 1) == (iota((blocks, blocks), 0) % n_col) * n_row + iota((blocks, blocks), 0) // n_col)
    lanes = con_pos.shape[1]
    con_high = dot((con // lanes).astype(F32).astype(BF16), perm, ((0,), (0,)))
    con_low = dot((con % lanes).astype(F32).astype(BF16), perm, ((0,), (0,)))
    table = ((con_pos[...] % PART) - PART // 2).astype(F32).astype(BF16)
    high_iota = iota((con_pos.shape[0], blocks), 0).astype(F32)
    low_iota = iota((lanes, blocks), 0).astype(F32)
    for t in range(count):
        picked = dot(table, flag(high_iota == con_high[t:t + 1, :]), ((0,), (0,)))
        local_pos[t:t + 1, :] = jnp.sum(jnp.where(low_iota == con_low[t:t + 1, :], picked, 0.0), axis=0, keepdims=True)

    wide_copy.wait()
    own_panel[...] = jnp.transpose(wide_v[...])[:TILE, :]

    own_x.wait()
    wait_bytes(x_v.at[pl.ds(0, order - chunk)], recv_sem.at[PRIMAL])
    own_slab = pltpu.make_async_copy(own_panel, slab_panel.at[my_tile], own_sem.at[SLAB])
    own_slab.start()
    to_col(SLAB, lambda peer: own_panel, slab_panel.at[my_tile])
    to_parts(PART_ROWS, lambda half: own_panel.at[:, pl.ds(half * PART, PART)], part_panel.at[my_tile])

    def lefts(part, _):
        a_copy(part).wait()
        for i in range(per_part):
            t = part * per_part + i
            left_v[t] = dot(x_v[...], a_v[t]).astype(BF16)

    lax.fori_loop(0, a_parts, lefts, None)

    own_s.wait()
    wait_bytes(s_v.at[pl.ds(0, order - chunk)], recv_sem.at[DUAL])
    total[...] = jnp.zeros_like(total)
    side = total.shape[0]

    def images(g, _):
        rows = pl.ds(pl.multiple_of(g * 16, 16), 16)
        image = dot(left_v[:, rows, :].reshape(count * 16, order), s_v[...]).reshape(count, 2, 8, order)
        coeff = a_v[:, rows, :].astype(F32).reshape(count, 2, 8, order)
        for h in range(2):
            total[...] += dot(
                coeff[:, h].reshape(side, order).astype(BF16), image[:, h].reshape(side, order).astype(BF16), ((1,), (1,))
            )

    lax.fori_loop(0, order // 16, images, None)

    per_row = count // n_row
    kept = jnp.where(iota((side, side), 0) % 8 == iota((side, side), 1) % 8, total[...], 0.0)
    by_slot = jnp.sum(kept.reshape(count, 8, side), axis=1)
    fold = jnp.where(iota((side, per_row * count), 1) % count == iota((side, per_row * count), 0) // 8, 1.0, 0.0)
    spread = dot(by_slot, fold, precision=lax.Precision.HIGHEST)
    spread = jnp.where(iota(spread.shape, 1) // count == iota(spread.shape, 0) % per_row, spread, 0.0)
    pack = jnp.where(iota((n_row, count), 1) // per_row == iota((n_row, count), 0), 1.0, 0.0)
    packed = dot(pack, spread, precision=lax.Precision.HIGHEST)
    entry_v[...] = packed
    gathered[pl.ds(row, 1)] = packed[None]

    def to_row(k, _):
        peer = lax.rem(row + k, n_row)
        send(entry_v, gathered.at[row], ENTRIES, peer, col)

    lax.fori_loop(1, n_row, to_row, None)
    wait_bytes(gathered.at[pl.ds(0, n_row - 1)], recv_sem.at[ENTRIES])
    every = gathered[...]
    chosen[...] = jnp.sum(jnp.where(iota(every.shape, 1) == row, every, 0.0), axis=1)
    own_entries = pltpu.make_async_copy(chosen, slab_entries.at[col], own_sem.at[3])
    own_entries.start()
    to_col(SLAB_ENTRIES, lambda peer: chosen, slab_entries.at[col])
    to_parts(PART_ENTRIES, lambda half: chosen, part_entries.at[col])

    own_slab.wait()
    wait_bytes(slab_panel.at[pl.ds(0, PW - TILE)], recv_sem.at[SLAB])
    wait_bytes(part_panel, recv_sem.at[PART_ROWS])
    wait_bytes(x_v.at[pl.ds(0, order - chunk)], send_sem.at[PRIMAL])
    wait_bytes(s_v.at[pl.ds(0, order - chunk)], send_sem.at[DUAL])
    wait_bytes(slab_panel.at[pl.ds(0, PW - TILE)], send_sem.at[SLAB])
    wait_parts_sent(PART_ROWS, part_panel, part_panel.at[pl.ds(0, PW - TILE)])
    wait_bytes(gathered.at[pl.ds(0, n_row - 1)], send_sem.at[ENTRIES])
    own_entries.wait()
    wait_bytes(slab_entries.at[pl.ds(0, n_col - 1)], recv_sem.at[SLAB_ENTRIES])
    wait_bytes(part_entries, recv_sem.at[PART_ENTRIES])
    wait_bytes(slab_entries.at[pl.ds(0, n_col - 1)], send_sem.at[SLAB_ENTRIES])
    wait_parts_sent(PART_ENTRIES, part_entries, part_entries.at[pl.ds(0, n_col - 1)])


def finish_kernel(
    n_row, n_col,
    schur_prev, slab_panel, part_panel, slab_entries, part_entries, local_pos, panel_inv,
    updated, panel_factor,
    added, inv_high, inv_low, other_high, other_low,
):
    step = pl.program_id(0)
    row = lax.axis_index("row")
    col = lax.axis_index("col")
    slots, blocks = local_pos.shape
    per_row = slots // n_row
    pos = local_pos[...]

    def slot_lanes(slot):
        return jnp.sum(jnp.where(iota(pos.shape, 0) == slot, pos, 0.0), axis=0, keepdims=True) + PART // 2

    @pl.when(step == 0)
    def _():
        pos16 = pos.astype(BF16)
        high, low = halves(panel_inv[...])
        inv_high[...] = high
        inv_low[...] = low
        key = iota((2 * blocks, PW), 0) % blocks
        tile = iota((2 * blocks, PW), 1) // TILE
        in_tile = []
        for u in range(2):
            pick = flag(iota((slots, PW), 0) == 2 * (iota((slots, PW), 1) // TILE) + u)
            local = dot(pos16, pick, ((0,), (0,)))
            in_tile.append(local == (iota((blocks, PW), 1) % TILE - PART // 2).astype(F32))

        def panel_terms(entries, s4):
            terms = [
                jnp.where(in_tile[u], dot(entries, flag(key == s4 * slots + 2 * tile + u)), 0.0) for u in range(2)
            ]
            return terms[0] + terms[1]

        own = jnp.concatenate(halves(slab_entries[...].reshape(blocks, -1)), axis=1)
        own_key = iota((2 * blocks, PART), 0) % blocks
        in_part = []
        for u in range(2):
            local = dot(pos16, flag(iota((slots, PART), 0) == 2 * col + u), ((0,), (0,)))
            in_part.append(local == (iota((blocks, PART), 1) - PART // 2).astype(F32))
        for s4 in range(per_row):
            here = pl.ds(s4 * blocks, blocks)
            there = pl.ds((per_row + s4) * blocks, blocks)
            high, low = halves(panel_terms(own, s4))
            added[here, 0:PW] = high
            added[there, 0:PW] = low
            terms = [
                jnp.where(in_part[u], dot(own, flag(own_key == s4 * slots + 2 * col + u)), 0.0) for u in range(2)
            ]
            high, low = halves(terms[0] + terms[1])
            added[here, PW:] = high
            added[there, PW:] = low

        other = jnp.concatenate(halves(part_entries[...].reshape(blocks, -1)), axis=1)
        panel = jnp.transpose(part_panel[...])
        for u in range(2):
            high, low = halves(panel_terms(other, 2 * lax.rem(col, n_col // n_row) + u))
            at = flag(iota((PART, blocks), 0).astype(F32) == slot_lanes(2 * col + u))
            panel += dot(at, high) + dot(at, low)
        high, low = halves(dot_halves(halves(panel), (inv_high[...], inv_low[...])))
        other_high[...] = high
        other_low[...] = low

    tall = updated.shape[0]
    at = []
    for s4 in range(per_row):
        place = slot_lanes(per_row * row + s4) + (s4 // 2) * PART
        at.append(flag((iota((tall, blocks), 0) + step * tall).astype(F32) == place))
    at = jnp.concatenate(at + at, axis=1)
    sums = dot(at, added[...])
    panel = jnp.transpose(slab_panel[...]) + sums[:, :PW]
    factor = dot_halves(halves(panel), (inv_high[...], inv_low[...]))
    panel_factor[...] = factor
    updated[...] = (
        schur_prev[...] + sums[:, PW:] - dot_halves(halves(factor), (other_high[...], other_low[...]), ((1,), (1,)))
    )


def per_device(n_row, n_col, moment_x, moment_s, coeffs, slot_con, con_pos, schur_prev, panel_inv):
    count, order = coeffs.shape[1], coeffs.shape[2]
    blocks = slot_con.shape[0]
    slab, part = schur_prev.shape
    vmem = pl.BlockSpec(memory_space=pltpu.VMEM)
    hbm = pl.BlockSpec(memory_space=pl.ANY)
    tile = (n_row, (count // n_row) * count)
    side = count * 8
    slab_panel, part_panel, slab_entries, part_entries, local_pos = pl.pallas_call(
        functools.partial(assemble_kernel, n_row, n_col),
        out_shape=(
            jax.ShapeDtypeStruct((PW, slab), F32),
            jax.ShapeDtypeStruct((PW, part), F32),
            jax.ShapeDtypeStruct((n_col,) + tile, F32),
            jax.ShapeDtypeStruct((n_col,) + tile, F32),
            jax.ShapeDtypeStruct((count, blocks), F32),
        ),
        in_specs=[hbm, hbm, hbm, vmem, vmem, hbm],
        out_specs=(hbm, hbm, hbm, hbm, vmem),
        scratch_shapes=[
            pltpu.VMEM((count, order, order), BF16),
            pltpu.VMEM((count, order, order), BF16),
            pltpu.VMEM((order, order), BF16),
            pltpu.VMEM((order, order), BF16),
            pltpu.VMEM((slab, 128), F32),
            pltpu.VMEM((TILE, slab), F32),
            pltpu.VMEM((side, side), F32),
            pltpu.VMEM(tile, F32),
            pltpu.VMEM((n_row,) + tile, F32),
            pltpu.VMEM(tile, F32),
            pltpu.SemaphoreType.DMA((8,)),
            pltpu.SemaphoreType.DMA((5,)),
            pltpu.SemaphoreType.DMA((7,)),
            pltpu.SemaphoreType.DMA((7,)),
        ],
        compiler_params=pltpu.CompilerParams(
            collective_id=0, has_side_effects=True, vmem_limit_bytes=56 * 2**20
        ),
    )(moment_x, moment_s, coeffs, slot_con, con_pos.reshape(-1, 128), schur_prev)

    steps = 4
    tall = slab // steps
    whole = lambda *shape: pl.BlockSpec(shape, lambda i: (0,) * len(shape))
    return pl.pallas_call(
        functools.partial(finish_kernel, n_row, n_col),
        grid=(steps,),
        out_shape=(jax.ShapeDtypeStruct((slab, part), F32), jax.ShapeDtypeStruct((slab, PW), F32)),
        in_specs=[
            pl.BlockSpec((tall, part), lambda i: (i, 0)),
            pl.BlockSpec((PW, tall), lambda i: (0, i)),
            whole(PW, part),
            whole(n_col, *tile),
            whole(n_col, *tile),
            whole(count, blocks),
            whole(PW, PW),
        ],
        out_specs=(pl.BlockSpec((tall, part), lambda i: (i, 0)), pl.BlockSpec((tall, PW), lambda i: (i, 0))),
        scratch_shapes=[
            pltpu.VMEM((2 * blocks * (count // n_row), PW + part), BF16),
            pltpu.VMEM((PW, PW), BF16),
            pltpu.VMEM((PW, PW), BF16),
            pltpu.VMEM((part, PW), BF16),
            pltpu.VMEM((part, PW), BF16),
        ],
        compiler_params=pltpu.CompilerParams(vmem_limit_bytes=48 * 2**20),
    )(schur_prev, slab_panel, part_panel, slab_entries, part_entries, local_pos, panel_inv)


def solution(mesh):
    placed = (
        P("row", "col", None),
        P("row", "col", None),
        P(("row", "col"), None, None, None),
        P(),
        P(),
        P("row", "col"),
        P(),
    )
    return jax.shard_map(
        functools.partial(per_device, mesh.shape["row"], mesh.shape["col"]),
        mesh=mesh,
        in_specs=placed,
        out_specs=(P("row", "col"), P("row", None)),
        check_vma=False,
    )
```

```python
import functools

import jax
import jax.numpy as jnp
from jax import lax
from jax.experimental import pallas as pl
from jax.experimental.pallas import tpu as pltpu
from jax.sharding import PartitionSpec as P

TILE = 16
PW = 256
PART = 512
MESH = pl.DeviceIdType.MESH
F32 = jnp.float32
BF16 = jnp.bfloat16
PRIMAL, DUAL, SLAB, SLAB_PASSED, PART_ROWS, ENTRIES, PAIRS = range(7)


def dot(a, b, dims=((1,), (0,)), precision=None):
    return lax.dot_general(a, b, (dims, ((), ())), precision=precision, preferred_element_type=F32)


def iota(shape, axis):
    return lax.broadcasted_iota(jnp.int32, shape, axis)


def halves(value):
    high = value.astype(BF16)
    return high, (value - high.astype(F32)).astype(BF16)


def dot_halves(a, b, dims=((1,), (0,))):
    a_high, a_low = a
    b_high, b_low = b
    return dot(a_high, b_high, dims) + dot(a_high, b_low, dims) + dot(a_low, b_high, dims)


def flag(condition):
    return jnp.where(condition, 1.0, 0.0).astype(BF16)


def assemble_kernel(
    n_row, n_col,
    moment_x, moment_s, coeffs, slot_con, con_pos, schur_prev,
    slab_panel, part_panel, entry_pairs, local_pos,
    a_v, left_v, x_v, s_v, wide_v, own_panel, total, image_v, entry_v, gathered, chosen,
    a_sem, own_sem, send_sem, recv_sem,
):
    row = lax.axis_index("row")
    col = lax.axis_index("col")
    count, order = a_v.shape[0], a_v.shape[1]
    chunk = order // n_col
    home = lax.div(col, n_col // n_row)

    a_parts = a_sem.shape[0]
    per_part = count // a_parts

    def a_copy(part):
        where = pl.ds(part * per_part, per_part)
        return pltpu.make_async_copy(coeffs.at[0, where], a_v.at[where], a_sem.at[part])

    my_chunk = pl.ds(pl.multiple_of(col * chunk, chunk), chunk)
    my_tile = pl.ds(pl.multiple_of(col * TILE, TILE), TILE)
    wide_copy = pltpu.make_async_copy(schur_prev.at[:, pl.ds(0, wide_v.shape[1])], wide_v, own_sem.at[4])
    own_x = pltpu.make_async_copy(moment_x.at[col], x_v.at[my_chunk], own_sem.at[PRIMAL])
    own_s = pltpu.make_async_copy(moment_s.at[col], s_v.at[my_chunk], own_sem.at[DUAL])
    wide_copy.start()
    own_x.start()
    own_s.start()
    lax.fori_loop(0, a_parts, lambda part, _: a_copy(part).start(), None)

    barrier = pltpu.get_barrier_semaphore()

    def greet(r, c):
        pl.semaphore_signal(barrier, inc=1, device_id=(r, c), device_id_type=MESH)

    lax.fori_loop(1, n_col, lambda k, _: greet(row, lax.rem(col + k, n_col)), None)
    lax.fori_loop(1, n_row, lambda k, _: greet(lax.rem(row + k, n_row), col), None)

    def greet_home(j, _):
        @pl.when(jnp.logical_or(home != row, j != col))
        def _():
            greet(home, j)

    lax.fori_loop(0, n_col, greet_home, None)
    at_home = home == row
    pl.semaphore_wait(barrier, n_col - 1 + n_row - 1 + n_col - at_home.astype(jnp.int32))

    def send(src, dst, which, r, c):
        pltpu.make_async_remote_copy(
            src_ref=src, dst_ref=dst, send_sem=send_sem.at[which], recv_sem=recv_sem.at[which],
            device_id=(r, c), device_id_type=MESH,
        ).start()

    def to_col(which, src, dst):
        def step(k, _):
            peer = lax.rem(col + k, n_col)
            send(src(peer), dst, which, row, peer)
        lax.fori_loop(1, n_col, step, None)

    halves_here = n_col // n_row

    def to_parts(which, src, dst):
        def step(k, _):
            r = lax.rem(row + k, n_row)
            for half in range(halves_here):
                c = row * halves_here + half

                @pl.when(jnp.logical_or(r != row, c != col))
                def _():
                    send(src(half), dst, which, r, c)

                @pl.when(jnp.logical_and(r == row, c == col))
                def _():
                    pltpu.make_async_copy(src(half), dst, recv_sem.at[which]).start()
        lax.fori_loop(0, n_row, step, None)

    def wait_bytes(ref, sem):
        pltpu.make_async_copy(ref, ref, sem).wait()

    def wait_parts_sent(which, whole, less):
        @pl.when(at_home)
        def _():
            wait_bytes(less, send_sem.at[which])

        @pl.when(jnp.logical_not(at_home))
        def _():
            wait_bytes(whole, send_sem.at[which])

    to_col(PRIMAL, lambda peer: moment_x.at[peer], x_v.at[my_chunk])
    to_col(DUAL, lambda peer: moment_s.at[peer], s_v.at[my_chunk])

    blocks = slot_con.shape[1]
    con = slot_con[...]
    perm = flag(iota((blocks, blocks), 1) == (iota((blocks, blocks), 0) % n_col) * n_row + iota((blocks, blocks), 0) // n_col)
    lanes = con_pos.shape[1]
    con_high = dot((con // lanes).astype(F32).astype(BF16), perm)
    con_low = dot((con % lanes).astype(F32).astype(BF16), perm)
    table = ((con_pos[...] % PART) - PART // 2).astype(F32).astype(BF16)
    high_iota = iota((con_pos.shape[0], blocks), 0).astype(F32)
    low_iota = iota((lanes, blocks), 0).astype(F32)
    for t in range(count):
        picked = dot(table, flag(high_iota == con_high[t:t + 1, :]), ((0,), (0,)))
        local_pos[t:t + 1, :] = jnp.sum(jnp.where(low_iota == con_low[t:t + 1, :], picked, 0.0), axis=0, keepdims=True)

    wide_copy.wait()
    own_panel[...] = jnp.transpose(wide_v[...])[:TILE, :]

    own_x.wait()
    wait_bytes(x_v.at[pl.ds(0, order - chunk)], recv_sem.at[PRIMAL])
    sibling = lax.bitwise_xor(col, 1)
    others = n_col // 2 - 1
    own_slab = pltpu.make_async_copy(own_panel, slab_panel.at[my_tile], own_sem.at[SLAB])
    own_slab.start()
    send(own_panel, slab_panel.at[my_tile], SLAB_PASSED, row, sibling)

    def to_chip(k, _):
        send(own_panel, slab_panel.at[my_tile], SLAB, row, lax.rem(col + 2 * k, n_col))

    lax.fori_loop(1, n_col // 2, to_chip, None)
    to_parts(PART_ROWS, lambda half: own_panel.at[:, pl.ds(half * PART, PART)], part_panel.at[my_tile])

    def lefts(part, _):
        a_copy(part).wait()
        for i in range(per_part):
            t = part * per_part + i
            left_v[:, t] = dot(x_v[...], a_v[t]).astype(BF16).reshape(groups, 16, order)

    groups = order // 16
    lax.fori_loop(0, a_parts, lefts, None)

    own_s.wait()
    wait_bytes(s_v.at[pl.ds(0, order - chunk)], recv_sem.at[DUAL])
    side = total.shape[0]
    total[...] = jnp.zeros_like(total)
    image_v[1] = jnp.zeros_like(image_v[1])

    def by_eights(value):
        value = value.reshape(count, 2, 8, order)
        return jnp.concatenate([value[:, h].reshape(side, order).astype(BF16) for h in range(2)], axis=1)

    def add_entries(g, slot):
        rows = pl.ds(pl.multiple_of(g * 16, 16), 16)
        total[...] += dot(by_eights(a_v[:, rows, :].astype(F32)), image_v[slot], ((1,), (1,)))

    unroll = 4

    def images(q, _):
        for i in range(unroll):
            g = q * unroll + i
            image = dot(left_v[g].reshape(count * 16, order), s_v[...])
            add_entries(jnp.maximum(g - 1, 0) if i == 0 else g - 1, (i + 1) % 2)
            image_v[i % 2] = by_eights(image)

    lax.fori_loop(0, groups // unroll // 2, images, None)

    wait_bytes(slab_panel.at[pl.ds(0, others * TILE)], recv_sem.at[SLAB])

    def pass_on(k, _):
        peer = lax.rem(col + 2 * k, n_col)
        tile = slab_panel.at[pl.ds(pl.multiple_of(peer * TILE, TILE), TILE)]
        send(tile, tile, SLAB_PASSED, row, sibling)

    lax.fori_loop(1, n_col // 2, pass_on, None)

    lax.fori_loop(groups // unroll // 2, groups // unroll, images, None)
    add_entries(groups - 1, 1)

    per_row = count // n_row
    kept = jnp.where(iota((side, side), 0) % 8 == iota((side, side), 1) % 8, total[...], 0.0)
    by_slot = jnp.sum(kept.reshape(count, 8, side), axis=1)
    fold = jnp.where(iota((side, per_row * count), 1) % count == iota((side, per_row * count), 0) // 8, 1.0, 0.0)
    spread = dot(by_slot, fold, precision=lax.Precision.HIGHEST)
    spread = jnp.where(iota(spread.shape, 1) // count == iota(spread.shape, 0) % per_row, spread, 0.0)
    pack = jnp.where(iota((n_row, count), 1) // per_row == iota((n_row, count), 0), 1.0, 0.0)
    packed = dot(pack, spread, precision=lax.Precision.HIGHEST)
    entry_v[...] = packed
    gathered[pl.ds(row, 1)] = packed[None]

    def to_row(k, _):
        peer = lax.rem(row + k, n_row)
        send(entry_v, gathered.at[row], ENTRIES, peer, col)

    lax.fori_loop(1, n_row, to_row, None)
    wait_bytes(gathered.at[pl.ds(0, n_row - 1)], recv_sem.at[ENTRIES])
    mine = jnp.sum(jnp.where(iota(gathered.shape, 1) == row, gathered[...], 0.0), axis=1)
    for q in range(n_row):
        chosen[q, 0] = mine
        chosen[q, 1] = gathered[:, q, :]
    own_entries = pltpu.make_async_copy(chosen.at[home], entry_pairs.at[col], own_sem.at[3])
    own_entries.start()
    to_col(PAIRS, lambda peer: chosen.at[lax.div(peer, n_col // n_row)], entry_pairs.at[col])

    own_slab.wait()
    wait_bytes(slab_panel.at[pl.ds(0, (others + 1) * TILE)], recv_sem.at[SLAB_PASSED])
    wait_bytes(part_panel, recv_sem.at[PART_ROWS])
    wait_bytes(x_v.at[pl.ds(0, order - chunk)], send_sem.at[PRIMAL])
    wait_bytes(s_v.at[pl.ds(0, order - chunk)], send_sem.at[DUAL])
    wait_bytes(slab_panel.at[pl.ds(0, others * TILE)], send_sem.at[SLAB])
    wait_bytes(slab_panel.at[pl.ds(0, (others + 1) * TILE)], send_sem.at[SLAB_PASSED])
    wait_parts_sent(PART_ROWS, part_panel, part_panel.at[pl.ds(0, PW - TILE)])
    wait_bytes(gathered.at[pl.ds(0, n_row - 1)], send_sem.at[ENTRIES])
    own_entries.wait()
    wait_bytes(entry_pairs.at[pl.ds(0, n_col - 1)], recv_sem.at[PAIRS])
    wait_bytes(entry_pairs.at[pl.ds(0, n_col - 1)], send_sem.at[PAIRS])


def finish_kernel(
    n_row, n_col,
    schur_prev, slab_panel, part_panel, entry_pairs, local_pos, panel_inv,
    updated, panel_factor,
    slab_v, part_v, pairs_v, pos_v, inv_v, updated_v, factor_v, added, in_sem, out_sem,
):
    loads = [
        pltpu.make_async_copy(src, dst, in_sem.at[k])
        for k, (src, dst) in enumerate(
            (
                (local_pos, pos_v), (entry_pairs, pairs_v), (part_panel, part_v), (panel_inv, inv_v),
                (slab_panel, slab_v), (schur_prev, updated_v),
            )
        )
    ]
    for load in loads:
        load.start()
    row = lax.axis_index("row")
    col = lax.axis_index("col")
    slots, blocks = local_pos.shape
    per_row = slots // n_row
    key = iota((2 * blocks, PW), 0) % blocks
    tile = iota((2 * blocks, PW), 1) // TILE
    own_key = iota((2 * blocks, PART), 0) % blocks
    loads[0].wait()
    pos = pos_v[...]
    pos16 = pos.astype(BF16)

    def slot_lanes(slot):
        return jnp.sum(jnp.where(iota(pos.shape, 0) == slot, pos, 0.0), axis=0, keepdims=True) + PART // 2

    in_tile, in_part = [], []
    for u in range(2):
        pick = flag(iota((slots, PW), 0) == 2 * (iota((slots, PW), 1) // TILE) + u)
        local = dot(pos16, pick, ((0,), (0,)))
        in_tile.append(local == (iota((blocks, PW), 1) % TILE - PART // 2).astype(F32))
        local = dot(pos16, flag(iota((slots, PART), 0) == 2 * col + u), ((0,), (0,)))
        in_part.append(local == (iota((blocks, PART), 1) - PART // 2).astype(F32))

    def panel_terms(entries, s4):
        terms = [jnp.where(in_tile[u], dot(entries, flag(key == s4 * slots + 2 * tile + u)), 0.0) for u in range(2)]
        return terms[0] + terms[1]

    loads[1].wait()
    own = jnp.concatenate(halves(pairs_v[:, 0].reshape(blocks, -1)), axis=1)
    for s4 in range(per_row):
        here = pl.ds(s4 * blocks, blocks)
        there = pl.ds((per_row + s4) * blocks, blocks)
        high, low = halves(panel_terms(own, s4))
        added[here, 0:PW] = high
        added[there, 0:PW] = low
        terms = [jnp.where(in_part[u], dot(own, flag(own_key == s4 * slots + 2 * col + u)), 0.0) for u in range(2)]
        high, low = halves(terms[0] + terms[1])
        added[here, PW:] = high
        added[there, PW:] = low

    other = jnp.concatenate(halves(pairs_v[:, 1].reshape(blocks, -1)), axis=1)
    loads[2].wait()
    panel = jnp.transpose(part_v[...])
    for u in range(2):
        high, low = halves(panel_terms(other, 2 * lax.rem(col, n_col // n_row) + u))
        at = flag(iota((PART, blocks), 0).astype(F32) == slot_lanes(2 * col + u))
        panel += dot(at, high) + dot(at, low)
    loads[3].wait()
    inverse = halves(inv_v[...])
    columns = halves(dot_halves(halves(panel), inverse))

    loads[4].wait()
    slab = schur_prev.shape[0]
    steps = out_sem.shape[1]
    tall = slab // steps
    writes = []
    for step in range(steps):
        rows = pl.ds(step * tall, tall)
        at = []
        for s4 in range(per_row):
            place = slot_lanes(per_row * row + s4) + (s4 // 2) * PART
            at.append(flag((iota((tall, blocks), 0) + step * tall).astype(F32) == place))
        sums = dot(jnp.concatenate(at + at, axis=1), added[...])
        panel = jnp.transpose(slab_v[:, rows]) + sums[:, :PW]
        factor = dot_halves(halves(panel), inverse)
        factor_v[rows] = factor
        writes.append(pltpu.make_async_copy(factor_v.at[rows], panel_factor.at[rows], out_sem.at[0, step]))
        writes[-1].start()
        if step == 0:
            loads[5].wait()
        updated_v[rows] = updated_v[rows] + sums[:, PW:] - dot_halves(halves(factor), columns, ((1,), (1,)))
        writes.append(pltpu.make_async_copy(updated_v.at[rows], updated.at[rows], out_sem.at[1, step]))
        writes[-1].start()
    for write in writes:
        write.wait()


def per_device(n_row, n_col, moment_x, moment_s, coeffs, slot_con, con_pos, schur_prev, panel_inv):
    count, order = coeffs.shape[1], coeffs.shape[2]
    blocks = slot_con.shape[0]
    slab, part = schur_prev.shape
    vmem = pl.BlockSpec(memory_space=pltpu.VMEM)
    hbm = pl.BlockSpec(memory_space=pltpu.HBM)
    tile = (n_row, (count // n_row) * count)
    side = count * 8
    slab_panel, part_panel, entry_pairs, local_pos = pl.pallas_call(
        functools.partial(assemble_kernel, n_row, n_col),
        out_shape=(
            jax.ShapeDtypeStruct((PW, slab), F32),
            jax.ShapeDtypeStruct((PW, part), F32),
            jax.ShapeDtypeStruct((n_col, 2) + tile, F32),
            jax.ShapeDtypeStruct((count, blocks), F32),
        ),
        in_specs=[hbm, hbm, hbm, vmem, vmem, hbm],
        out_specs=(hbm, hbm, hbm, vmem),
        scratch_shapes=[
            pltpu.VMEM((count, order, order), BF16),
            pltpu.VMEM((order // 16, count, 16, order), BF16),
            pltpu.VMEM((order, order), BF16),
            pltpu.VMEM((order, order), BF16),
            pltpu.VMEM((slab, 128), F32),
            pltpu.VMEM((TILE, slab), F32),
            pltpu.VMEM((side, side), F32),
            pltpu.VMEM((2, side, 2 * order), BF16),
            pltpu.VMEM(tile, F32),
            pltpu.VMEM((n_row,) + tile, F32),
            pltpu.VMEM((n_row, 2) + tile, F32),
            pltpu.SemaphoreType.DMA((4,)),
            pltpu.SemaphoreType.DMA((5,)),
            pltpu.SemaphoreType.DMA((7,)),
            pltpu.SemaphoreType.DMA((7,)),
        ],
        compiler_params=pltpu.CompilerParams(
            collective_id=0, has_side_effects=True, vmem_limit_bytes=54 * 2**20
        ),
    )(moment_x, moment_s, coeffs, slot_con.T, con_pos.reshape(-1, 128), schur_prev)

    steps = 4
    return pl.pallas_call(
        functools.partial(finish_kernel, n_row, n_col),
        out_shape=(jax.ShapeDtypeStruct((slab, part), F32), jax.ShapeDtypeStruct((slab, PW), F32)),
        in_specs=[hbm] * 6,
        out_specs=(hbm, hbm),
        scratch_shapes=[
            pltpu.VMEM((PW, slab), F32),
            pltpu.VMEM((PW, part), F32),
            pltpu.VMEM((n_col, 2) + tile, F32),
            pltpu.VMEM((count, blocks), F32),
            pltpu.VMEM((PW, PW), F32),
            pltpu.VMEM((slab, part), F32),
            pltpu.VMEM((slab, PW), F32),
            pltpu.VMEM((2 * blocks * (count // n_row), PW + part), BF16),
            pltpu.SemaphoreType.DMA((6,)),
            pltpu.SemaphoreType.DMA((2, steps)),
        ],
        compiler_params=pltpu.CompilerParams(vmem_limit_bytes=63 * 2**20),
    )(schur_prev, slab_panel, part_panel, entry_pairs, local_pos, panel_inv)


def solution(mesh):
    placed = (
        P("row", "col", None),
        P("row", "col", None),
        P(("row", "col"), None, None, None),
        P(),
        P(),
        P("row", "col"),
        P(),
    )
    return jax.shard_map(
        functools.partial(per_device, mesh.shape["row"], mesh.shape["col"]),
        mesh=mesh,
        in_specs=placed,
        out_specs=(P("row", "col"), P("row", None)),
        check_vma=False,
    )
```

```python
import functools

import jax
import jax.numpy as jnp
from jax import lax
from jax.experimental import pallas as pl
from jax.experimental.pallas import tpu as pltpu
from jax.sharding import PartitionSpec as P

TILE = 16
PW = 256
PART = 512
MESH = pl.DeviceIdType.MESH
F32 = jnp.float32
BF16 = jnp.bfloat16
PRIMAL, DUAL, SLAB, SLAB_PASSED, PART_ROWS, PAIRS = range(6)


def dot(a, b, dims=((1,), (0,)), precision=None):
    return lax.dot_general(a, b, (dims, ((), ())), precision=precision, preferred_element_type=F32)


def iota(shape, axis):
    return lax.broadcasted_iota(jnp.int32, shape, axis)


def halves(value):
    high = value.astype(BF16)
    return high, (value - high.astype(F32)).astype(BF16)


def dot_halves(a, b, dims=((1,), (0,))):
    a_high, a_low = a
    b_high, b_low = b
    return dot(a_high, b_high, dims) + dot(a_high, b_low, dims) + dot(a_low, b_high, dims)


def flag(condition):
    return jnp.where(condition, 1.0, 0.0).astype(BF16)


def assemble_kernel(
    n_row, n_col,
    moment_x, moment_s, coeffs, slot_con, con_pos, schur_prev,
    slab_panel, part_panel, entry_pairs, local_pos,
    a_v, left_v, x_v, s_v, wide_v, own_panel, total, image_v, chosen,
    a_sem, own_sem, send_sem, recv_sem, everyone,
):
    row = lax.axis_index("row")
    col = lax.axis_index("col")
    count, order = a_v.shape[0], a_v.shape[1]
    chunk = order // n_col
    home = lax.div(col, n_col // n_row)

    a_parts = a_sem.shape[0]
    per_part = count // a_parts

    def a_copy(part):
        where = pl.ds(part * per_part, per_part)
        return pltpu.make_async_copy(coeffs.at[0, where], a_v.at[where], a_sem.at[part])

    my_chunk = pl.ds(pl.multiple_of(col * chunk, chunk), chunk)
    my_tile = pl.ds(pl.multiple_of(col * TILE, TILE), TILE)
    wide_copy = pltpu.make_async_copy(schur_prev.at[:, pl.ds(0, wide_v.shape[1])], wide_v, own_sem.at[4])
    own_x = pltpu.make_async_copy(moment_x.at[col], x_v.at[my_chunk], own_sem.at[PRIMAL])
    own_s = pltpu.make_async_copy(moment_s.at[col], s_v.at[my_chunk], own_sem.at[DUAL])
    wide_copy.start()
    own_x.start()
    own_s.start()
    lax.fori_loop(0, a_parts, lambda part, _: a_copy(part).start(), None)

    barrier = pltpu.get_barrier_semaphore()

    def greet(r, c):
        pl.semaphore_signal(barrier, inc=1, device_id=(r, c), device_id_type=MESH)

    lax.fori_loop(1, n_col, lambda k, _: greet(row, lax.rem(col + k, n_col)), None)
    lax.fori_loop(1, n_row, lambda k, _: greet(lax.rem(row + k, n_row), col), None)

    at_home = home == row
    pl.semaphore_wait(barrier, n_col - 1 + n_row - 1)

    def all_here(k, _):
        pl.semaphore_signal(everyone, inc=1, device_id=(lax.rem(row + k, n_row), col), device_id_type=MESH)

    def send(src, dst, which, r, c):
        pltpu.make_async_remote_copy(
            src_ref=src, dst_ref=dst, send_sem=send_sem.at[which], recv_sem=recv_sem.at[which],
            device_id=(r, c), device_id_type=MESH,
        ).start()

    def to_col(which, src, dst):
        def step(k, _):
            peer = lax.rem(col + k, n_col)
            send(src(peer), dst, which, row, peer)
        lax.fori_loop(1, n_col, step, None)

    halves_here = n_col // n_row

    def to_parts(which, src, dst):
        def step(k, _):
            r = lax.rem(row + k, n_row)
            for half in range(halves_here):
                c = row * halves_here + half

                @pl.when(jnp.logical_or(r != row, c != col))
                def _():
                    send(src(half), dst, which, r, c)

                @pl.when(jnp.logical_and(r == row, c == col))
                def _():
                    pltpu.make_async_copy(src(half), dst, recv_sem.at[which]).start()
        lax.fori_loop(0, n_row, step, None)

    def wait_bytes(ref, sem):
        pltpu.make_async_copy(ref, ref, sem).wait()

    def wait_parts_sent(which, whole, less):
        @pl.when(at_home)
        def _():
            wait_bytes(less, send_sem.at[which])

        @pl.when(jnp.logical_not(at_home))
        def _():
            wait_bytes(whole, send_sem.at[which])

    to_col(PRIMAL, lambda peer: moment_x.at[peer], x_v.at[my_chunk])
    lax.fori_loop(1, n_row, all_here, None)

    blocks = slot_con.shape[1]
    con = slot_con[...]
    perm = flag(iota((blocks, blocks), 1) == (iota((blocks, blocks), 0) % n_col) * n_row + iota((blocks, blocks), 0) // n_col)
    lanes = con_pos.shape[1]
    con_high = dot((con // lanes).astype(F32).astype(BF16), perm)
    con_low = dot((con % lanes).astype(F32).astype(BF16), perm)
    table = ((con_pos[...] % PART) - PART // 2).astype(F32).astype(BF16)
    high_iota = iota((con_pos.shape[0], blocks), 0).astype(F32)
    low_iota = iota((lanes, blocks), 0).astype(F32)
    for t in range(count):
        picked = dot(table, flag(high_iota == con_high[t:t + 1, :]), ((0,), (0,)))
        local_pos[t:t + 1, :] = jnp.sum(jnp.where(low_iota == con_low[t:t + 1, :], picked, 0.0), axis=0, keepdims=True)

    wait_bytes(x_v.at[pl.ds(0, order - chunk)], send_sem.at[PRIMAL])
    to_col(DUAL, lambda peer: moment_s.at[peer], s_v.at[my_chunk])

    wide_copy.wait()
    own_panel[...] = jnp.transpose(wide_v[...])[:TILE, :]

    own_x.wait()
    wait_bytes(x_v.at[pl.ds(0, order - chunk)], recv_sem.at[PRIMAL])
    def lefts(part, _):
        a_copy(part).wait()
        for i in range(per_part):
            t = part * per_part + i
            left_v[:, t] = dot(x_v[...], a_v[t]).astype(BF16).reshape(groups, 16, order)

    groups = order // 16
    lax.fori_loop(0, a_parts, lefts, None)

    own_s.wait()
    wait_bytes(s_v.at[pl.ds(0, order - chunk)], recv_sem.at[DUAL])
    pl.semaphore_wait(everyone, n_row - 1)

    sibling = lax.bitwise_xor(col, 1)
    others = n_col // 2 - 1
    own_slab = pltpu.make_async_copy(own_panel, slab_panel.at[my_tile], own_sem.at[SLAB])
    own_slab.start()
    send(own_panel, slab_panel.at[my_tile], SLAB_PASSED, row, sibling)

    def to_chip(k, _):
        send(own_panel, slab_panel.at[my_tile], SLAB, row, lax.rem(col + 2 * k, n_col))

    lax.fori_loop(1, n_col // 2, to_chip, None)
    to_parts(PART_ROWS, lambda half: own_panel.at[:, pl.ds(half * PART, PART)], part_panel.at[my_tile])

    side = total.shape[0]
    per_row = count // n_row
    total[...] = jnp.zeros_like(total)
    image_v[1] = jnp.zeros_like(image_v[1])

    def by_eights(value):
        value = value.reshape(count, 2, 8, order)
        return jnp.concatenate([value[:, h].reshape(side, order).astype(BF16) for h in range(2)], axis=1)

    def add_entries(g, slot):
        rows = pl.ds(pl.multiple_of(g * 16, 16), 16)
        coeff = a_v[:, rows, :].astype(F32).reshape(n_row, per_row, 16, order)
        coeff = jnp.transpose(coeff, (1, 0, 2, 3)).reshape(count, 16, order)
        total[...] += dot(by_eights(coeff), image_v[slot], ((1,), (1,)))

    unroll = 4

    def images(q, _):
        for i in range(unroll):
            g = q * unroll + i
            image = dot(left_v[g].reshape(count * 16, order), s_v[...])
            add_entries(jnp.maximum(g - 1, 0) if i == 0 else g - 1, (i + 1) % 2)
            image_v[i % 2] = by_eights(image)

    lax.fori_loop(0, groups // unroll * 3 // 4, images, None)

    wait_bytes(slab_panel.at[pl.ds(0, others * TILE)], recv_sem.at[SLAB])

    def pass_on(k, _):
        peer = lax.rem(col + 2 * k, n_col)
        tile = slab_panel.at[pl.ds(pl.multiple_of(peer * TILE, TILE), TILE)]
        send(tile, tile, SLAB_PASSED, row, sibling)

    lax.fori_loop(1, n_col // 2, pass_on, None)

    lax.fori_loop(groups // unroll * 3 // 4, groups // unroll, images, None)
    add_entries(groups - 1, 1)

    kept = jnp.where(iota((side, side), 0) % 8 == iota((side, side), 1) % 8, total[...], 0.0)
    by_slot = jnp.concatenate(halves(jnp.sum(kept.reshape(count, 8, side), axis=1)), axis=1)
    spread = dot(by_slot, flag(iota((2 * side, per_row * count), 1) % count == iota((2 * side, per_row * count), 0) % side // 8))
    packed = jnp.zeros((n_row, per_row * count), F32)
    for s4 in range(per_row):
        mine = spread[s4 * n_row:(s4 + 1) * n_row]
        packed += jnp.where(iota(mine.shape, 1) // count == s4, mine, 0.0)
    for i in range(n_row):
        same = jnp.broadcast_to(packed[i:i + 1], packed.shape)
        chosen[i, :, 0, :] = same
        chosen[:, i, 1, :] = same

    my_block = col * n_row + row
    own_entries = pltpu.make_async_copy(chosen.at[row, home], entry_pairs.at[my_block], own_sem.at[3])
    own_entries.start()

    def away(j):
        return jnp.where(j < 2, j + 2, 3 - j)

    def to_all(k, _):
        y = away(lax.rem(lax.div(k, 2), 4))
        dx = away(lax.div(k, 32)) * 2 + lax.div(y, 2)
        dz = away(lax.rem(lax.div(k, 8), 4)) * 4 + lax.rem(y, 2) * 2 + 1 - lax.rem(k, 2)
        r = lax.bitwise_xor(row, dx)
        c = lax.bitwise_xor(col, dz)
        send(chosen.at[r, lax.div(c, n_col // n_row)], entry_pairs.at[my_block], PAIRS, r, c)

    every = n_row * n_col
    lax.fori_loop(0, every - 1, to_all, None)

    own_slab.wait()
    wait_bytes(slab_panel.at[pl.ds(0, (others + 1) * TILE)], recv_sem.at[SLAB_PASSED])
    wait_bytes(part_panel, recv_sem.at[PART_ROWS])
    wait_bytes(s_v.at[pl.ds(0, order - chunk)], send_sem.at[DUAL])
    wait_bytes(slab_panel.at[pl.ds(0, others * TILE)], send_sem.at[SLAB])
    wait_bytes(slab_panel.at[pl.ds(0, (others + 1) * TILE)], send_sem.at[SLAB_PASSED])
    wait_parts_sent(PART_ROWS, part_panel, part_panel.at[pl.ds(0, PW - TILE)])
    own_entries.wait()
    wait_bytes(entry_pairs.at[pl.ds(0, every - 1)], recv_sem.at[PAIRS])
    wait_bytes(entry_pairs.at[pl.ds(0, every - 1)], send_sem.at[PAIRS])


def finish_kernel(
    n_row, n_col,
    schur_prev, slab_panel, part_panel, entry_pairs, local_pos, panel_inv,
    updated, panel_factor,
    slab_v, part_v, pairs_v, pos_v, inv_v, updated_v, factor_v, added, in_sem, out_sem,
):
    loads = [
        pltpu.make_async_copy(src, dst, in_sem.at[k])
        for k, (src, dst) in enumerate(
            (
                (local_pos, pos_v), (entry_pairs, pairs_v), (part_panel, part_v), (panel_inv, inv_v),
                (slab_panel, slab_v), (schur_prev, updated_v),
            )
        )
    ]
    for load in loads:
        load.start()
    row = lax.axis_index("row")
    col = lax.axis_index("col")
    slots, blocks = local_pos.shape
    per_row = slots // n_row
    key = iota((2 * blocks, PW), 0) % blocks
    tile = iota((2 * blocks, PW), 1) // TILE
    own_key = iota((2 * blocks, PART), 0) % blocks
    loads[0].wait()
    pos = pos_v[...]
    pos16 = pos.astype(BF16)

    def slot_lanes(slot):
        return jnp.sum(jnp.where(iota(pos.shape, 0) == slot, pos, 0.0), axis=0, keepdims=True) + PART // 2

    in_tile, in_part = [], []
    for u in range(2):
        pick = flag(iota((slots, PW), 0) == 2 * (iota((slots, PW), 1) // TILE) + u)
        local = dot(pos16, pick, ((0,), (0,)))
        in_tile.append(local == (iota((blocks, PW), 1) % TILE - PART // 2).astype(F32))
        local = dot(pos16, flag(iota((slots, PART), 0) == 2 * col + u), ((0,), (0,)))
        in_part.append(local == (iota((blocks, PART), 1) - PART // 2).astype(F32))

    def panel_terms(entries, s4):
        terms = [jnp.where(in_tile[u], dot(entries, flag(key == s4 * slots + 2 * tile + u)), 0.0) for u in range(2)]
        return terms[0] + terms[1]

    loads[1].wait()
    own = jnp.concatenate(halves(pairs_v[pl.ds(0, blocks, stride=2), :]), axis=1)
    for s4 in range(per_row):
        here = pl.ds(s4 * blocks, blocks)
        there = pl.ds((per_row + s4) * blocks, blocks)
        high, low = halves(panel_terms(own, s4))
        added[here, 0:PW] = high
        added[there, 0:PW] = low
        terms = [jnp.where(in_part[u], dot(own, flag(own_key == s4 * slots + 2 * col + u)), 0.0) for u in range(2)]
        high, low = halves(terms[0] + terms[1])
        added[here, PW:] = high
        added[there, PW:] = low

    other = jnp.concatenate(halves(pairs_v[pl.ds(1, blocks, stride=2), :]), axis=1)
    loads[2].wait()
    panel = jnp.transpose(part_v[...])
    for u in range(2):
        high, low = halves(panel_terms(other, 2 * lax.rem(col, n_col // n_row) + u))
        at = flag(iota((PART, blocks), 0).astype(F32) == slot_lanes(2 * col + u))
        panel += dot(at, high) + dot(at, low)
    loads[3].wait()
    inverse = halves(inv_v[...])
    columns = halves(dot_halves(halves(panel), inverse))

    loads[4].wait()
    slab = schur_prev.shape[0]
    steps = out_sem.shape[1]
    tall = slab // steps
    writes = []
    for step in range(steps):
        rows = pl.ds(step * tall, tall)
        at = []
        for s4 in range(per_row):
            place = slot_lanes(per_row * row + s4) + (s4 // 2) * PART
            at.append(flag((iota((tall, blocks), 0) + step * tall).astype(F32) == place))
        sums = dot(jnp.concatenate(at + at, axis=1), added[...])
        panel = jnp.transpose(slab_v[:, rows]) + sums[:, :PW]
        factor = dot_halves(halves(panel), inverse)
        factor_v[rows] = factor
        writes.append(pltpu.make_async_copy(factor_v.at[rows], panel_factor.at[rows], out_sem.at[0, step]))
        writes[-1].start()
        if step == 0:
            loads[5].wait()
        updated_v[rows] = updated_v[rows] + sums[:, PW:] - dot_halves(halves(factor), columns, ((1,), (1,)))
        writes.append(pltpu.make_async_copy(updated_v.at[rows], updated.at[rows], out_sem.at[1, step]))
        writes[-1].start()
    for write in writes:
        write.wait()


def per_device(n_row, n_col, moment_x, moment_s, coeffs, slot_con, con_pos, schur_prev, panel_inv):
    count, order = coeffs.shape[1], coeffs.shape[2]
    blocks = slot_con.shape[0]
    slab, part = schur_prev.shape
    vmem = pl.BlockSpec(memory_space=pltpu.VMEM)
    hbm = pl.BlockSpec(memory_space=pltpu.HBM)
    lanes = (count // n_row) * count
    side = count * 8
    slab_panel, part_panel, entry_pairs, local_pos = pl.pallas_call(
        functools.partial(assemble_kernel, n_row, n_col),
        out_shape=(
            jax.ShapeDtypeStruct((PW, slab), F32),
            jax.ShapeDtypeStruct((PW, part), F32),
            jax.ShapeDtypeStruct((blocks, 2, lanes), F32),
            jax.ShapeDtypeStruct((count, blocks), F32),
        ),
        in_specs=[hbm, hbm, hbm, vmem, vmem, hbm],
        out_specs=(hbm, hbm, hbm, vmem),
        scratch_shapes=[
            pltpu.VMEM((count, order, order), BF16),
            pltpu.VMEM((order // 16, count, 16, order), BF16),
            pltpu.VMEM((order, order), BF16),
            pltpu.VMEM((order, order), BF16),
            pltpu.VMEM((slab, 128), F32),
            pltpu.VMEM((TILE, slab), F32),
            pltpu.VMEM((side, side), F32),
            pltpu.VMEM((2, side, 2 * order), BF16),
            pltpu.VMEM((n_row, n_row, 2, lanes), F32),
            pltpu.SemaphoreType.DMA((4,)),
            pltpu.SemaphoreType.DMA((5,)),
            pltpu.SemaphoreType.DMA((6,)),
            pltpu.SemaphoreType.DMA((6,)),
            pltpu.SemaphoreType.REGULAR,
        ],
        compiler_params=pltpu.CompilerParams(
            collective_id=0, has_side_effects=True, vmem_limit_bytes=54 * 2**20
        ),
    )(moment_x, moment_s, coeffs, slot_con.T, con_pos.reshape(-1, 128), schur_prev)

    steps = 4
    return pl.pallas_call(
        functools.partial(finish_kernel, n_row, n_col),
        out_shape=(jax.ShapeDtypeStruct((slab, part), F32), jax.ShapeDtypeStruct((slab, PW), F32)),
        in_specs=[hbm] * 6,
        out_specs=(hbm, hbm),
        scratch_shapes=[
            pltpu.VMEM((PW, slab), F32),
            pltpu.VMEM((PW, part), F32),
            pltpu.VMEM((2 * blocks, lanes), F32),
            pltpu.VMEM((count, blocks), F32),
            pltpu.VMEM((PW, PW), F32),
            pltpu.VMEM((slab, part), F32),
            pltpu.VMEM((slab, PW), F32),
            pltpu.VMEM((2 * blocks * (count // n_row), PW + part), BF16),
            pltpu.SemaphoreType.DMA((6,)),
            pltpu.SemaphoreType.DMA((2, steps)),
        ],
        compiler_params=pltpu.CompilerParams(vmem_limit_bytes=63 * 2**20),
    )(schur_prev, slab_panel, part_panel, entry_pairs.reshape(2 * blocks, lanes), local_pos, panel_inv)


def solution(mesh):
    placed = (
        P("row", "col", None),
        P("row", "col", None),
        P(("row", "col"), None, None, None),
        P(),
        P(),
        P("row", "col"),
        P(),
    )
    return jax.shard_map(
        functools.partial(per_device, mesh.shape["row"], mesh.shape["col"]),
        mesh=mesh,
        in_specs=placed,
        out_specs=(P("row", "col"), P("row", None)),
        check_vma=False,
    )
```

```python
import functools

import jax
import jax.numpy as jnp
from jax import lax
from jax.experimental import pallas as pl
from jax.experimental.pallas import tpu as pltpu
from jax.sharding import PartitionSpec as P

TILE = 16
PW = 256
PART = 512
MESH = pl.DeviceIdType.MESH
F32 = jnp.float32
BF16 = jnp.bfloat16
PRIMAL, DUAL, SLAB, SLAB_PASSED, PART_ROWS, PAIRS = range(6)


def dot(a, b, dims=((1,), (0,)), precision=None):
    return lax.dot_general(a, b, (dims, ((), ())), precision=precision, preferred_element_type=F32)


def iota(shape, axis):
    return lax.broadcasted_iota(jnp.int32, shape, axis)


def halves(value):
    high = value.astype(BF16)
    return high, (value - high.astype(F32)).astype(BF16)


def dot_halves(a, b, dims=((1,), (0,))):
    a_high, a_low = a
    b_high, b_low = b
    return dot(a_high, b_high, dims) + dot(a_high, b_low, dims) + dot(a_low, b_high, dims)


def flag(condition):
    return jnp.where(condition, 1.0, 0.0).astype(BF16)


def assemble_kernel(
    n_row, n_col,
    moment_x, moment_s, coeffs, slot_con, con_pos, schur_prev, panel_inv,
    slab_factor, part_factor, entry_pairs, local_pos,
    slab_panel, part_panel, a_v, left_v, x_v, s_v, wide_v, own_panel, total, image_v, chosen,
    a_sem, own_sem, send_sem, recv_sem, everyone,
):
    row = lax.axis_index("row")
    col = lax.axis_index("col")
    count, order = a_v.shape[0], a_v.shape[1]
    chunk = order // n_col
    home = lax.div(col, n_col // n_row)

    a_parts = a_sem.shape[0]
    per_part = count // a_parts

    def a_copy(part):
        where = pl.ds(part * per_part, per_part)
        return pltpu.make_async_copy(coeffs.at[0, where], a_v.at[where], a_sem.at[part])

    my_chunk = pl.ds(pl.multiple_of(col * chunk, chunk), chunk)
    my_tile = pl.ds(pl.multiple_of(col * TILE, TILE), TILE)
    wide_copy = pltpu.make_async_copy(schur_prev.at[:, pl.ds(0, wide_v.shape[1])], wide_v, own_sem.at[4])
    own_x = pltpu.make_async_copy(moment_x.at[col], x_v.at[my_chunk], own_sem.at[PRIMAL])
    own_s = pltpu.make_async_copy(moment_s.at[col], s_v.at[my_chunk], own_sem.at[DUAL])
    wide_copy.start()
    own_x.start()
    own_s.start()
    lax.fori_loop(0, a_parts, lambda part, _: a_copy(part).start(), None)

    barrier = pltpu.get_barrier_semaphore()

    def greet(r, c):
        pl.semaphore_signal(barrier, inc=1, device_id=(r, c), device_id_type=MESH)

    lax.fori_loop(1, n_row, lambda k, _: greet(lax.rem(row + k, n_row), col), None)
    lax.fori_loop(1, n_col, lambda k, _: greet(row, lax.rem(col + k, n_col)), None)

    at_home = home == row
    pl.semaphore_wait(barrier, n_col - 1 + n_row - 1)

    def all_here(k, _):
        pl.semaphore_signal(everyone, inc=1, device_id=(lax.rem(row + k, n_row), col), device_id_type=MESH)

    def send(src, dst, which, r, c):
        pltpu.make_async_remote_copy(
            src_ref=src, dst_ref=dst, send_sem=send_sem.at[which], recv_sem=recv_sem.at[which],
            device_id=(r, c), device_id_type=MESH,
        ).start()

    def to_col(which, src, dst):
        def step(k, _):
            peer = lax.rem(col + k, n_col)
            send(src(peer), dst, which, row, peer)
        lax.fori_loop(1, n_col, step, None)

    halves_here = n_col // n_row

    def to_parts(which, src, dst):
        def step(k, _):
            r = lax.rem(row + k, n_row)
            for half in range(halves_here):
                c = row * halves_here + half

                @pl.when(jnp.logical_or(r != row, c != col))
                def _():
                    send(src(half), dst, which, r, c)

                @pl.when(jnp.logical_and(r == row, c == col))
                def _():
                    pltpu.make_async_copy(src(half), dst, recv_sem.at[which]).start()
        lax.fori_loop(0, n_row, step, None)

    def wait_bytes(ref, sem):
        pltpu.make_async_copy(ref, ref, sem).wait()

    def wait_parts_sent(which, whole, less):
        @pl.when(at_home)
        def _():
            wait_bytes(less, send_sem.at[which])

        @pl.when(jnp.logical_not(at_home))
        def _():
            wait_bytes(whole, send_sem.at[which])

    to_col(PRIMAL, lambda peer: moment_x.at[peer], x_v.at[my_chunk])
    lax.fori_loop(1, n_row, all_here, None)

    blocks = slot_con.shape[1]
    con = slot_con[...]
    perm = flag(iota((blocks, blocks), 1) == (iota((blocks, blocks), 0) % n_col) * n_row + iota((blocks, blocks), 0) // n_col)
    lanes = con_pos.shape[1]
    con_high = dot((con // lanes).astype(F32).astype(BF16), perm)
    con_low = dot((con % lanes).astype(F32).astype(BF16), perm)
    table = ((con_pos[...] % PART) - PART // 2).astype(F32).astype(BF16)
    high_iota = iota((con_pos.shape[0], blocks), 0).astype(F32)
    low_iota = iota((lanes, blocks), 0).astype(F32)
    for t in range(count):
        picked = dot(table, flag(high_iota == con_high[t:t + 1, :]), ((0,), (0,)))
        local_pos[t:t + 1, :] = jnp.sum(jnp.where(low_iota == con_low[t:t + 1, :], picked, 0.0), axis=0, keepdims=True)

    wait_bytes(x_v.at[pl.ds(0, order - chunk)], send_sem.at[PRIMAL])
    to_col(DUAL, lambda peer: moment_s.at[peer], s_v.at[my_chunk])

    wide_copy.wait()
    own_panel[...] = jnp.transpose(wide_v[...])[:TILE, :]

    own_x.wait()
    wait_bytes(x_v.at[pl.ds(0, order - chunk)], recv_sem.at[PRIMAL])
    def lefts(part, _):
        a_copy(part).wait()
        for i in range(per_part):
            t = part * per_part + i
            left_v[:, t] = dot(x_v[...], a_v[t]).astype(BF16).reshape(groups, 16, order)

    groups = order // 16
    lax.fori_loop(0, a_parts // 2, lefts, None)
    pl.semaphore_wait(everyone, n_row - 1)

    sibling = lax.bitwise_xor(col, 1)
    others = n_col // 2 - 1
    own_slab = pltpu.make_async_copy(own_panel, slab_panel.at[my_tile], own_sem.at[SLAB])
    own_slab.start()
    send(own_panel, slab_panel.at[my_tile], SLAB_PASSED, row, sibling)

    def to_chip(k, _):
        send(own_panel, slab_panel.at[my_tile], SLAB, row, lax.rem(col + 2 * k, n_col))

    lax.fori_loop(1, n_col // 2, to_chip, None)
    to_parts(PART_ROWS, lambda half: own_panel.at[:, pl.ds(half * PART, PART)], part_panel.at[my_tile])

    lax.fori_loop(a_parts // 2, a_parts, lefts, None)

    own_s.wait()
    wait_bytes(s_v.at[pl.ds(0, order - chunk)], recv_sem.at[DUAL])
    side = total.shape[0]
    per_row = count // n_row
    total[...] = jnp.zeros_like(total)
    image_v[1] = jnp.zeros_like(image_v[1])

    def by_eights(value):
        value = value.reshape(count, 2, 8, order)
        return jnp.concatenate([value[:, h].reshape(side, order).astype(BF16) for h in range(2)], axis=1)

    def add_entries(g, slot):
        rows = pl.ds(pl.multiple_of(g * 16, 16), 16)
        coeff = a_v[:, rows, :].astype(F32).reshape(n_row, per_row, 16, order)
        coeff = jnp.transpose(coeff, (1, 0, 2, 3)).reshape(count, 16, order)
        total[...] += dot(by_eights(coeff), image_v[slot], ((1,), (1,)))

    unroll = 8

    def images(q, _):
        for i in range(unroll):
            g = q * unroll + i
            image = dot(left_v[g].reshape(count * 16, order), s_v[...])
            add_entries(jnp.maximum(g - 1, 0) if i == 0 else g - 1, (i + 1) % 2)
            image_v[i % 2] = by_eights(image)

    lax.fori_loop(0, groups // unroll * 3 // 4, images, None)

    wait_bytes(slab_panel.at[pl.ds(0, others * TILE)], recv_sem.at[SLAB])

    def pass_on(k, _):
        peer = lax.rem(col + 2 * k, n_col)
        tile = slab_panel.at[pl.ds(pl.multiple_of(peer * TILE, TILE), TILE)]
        send(tile, tile, SLAB_PASSED, row, sibling)

    lax.fori_loop(1, n_col // 2, pass_on, None)

    lax.fori_loop(groups // unroll * 3 // 4, groups // unroll, images, None)
    add_entries(groups - 1, 1)

    kept = jnp.where(iota((side, side), 0) % 8 == iota((side, side), 1) % 8, total[...], 0.0)
    by_slot = jnp.concatenate(halves(jnp.sum(kept.reshape(count, 8, side), axis=1)), axis=1)
    spread = dot(by_slot, flag(iota((2 * side, per_row * count), 1) % count == iota((2 * side, per_row * count), 0) % side // 8))
    packed = jnp.zeros((n_row, per_row * count), F32)
    for s4 in range(per_row):
        mine = spread[s4 * n_row:(s4 + 1) * n_row]
        packed += jnp.where(iota(mine.shape, 1) // count == s4, mine, 0.0)
    for i in range(n_row):
        same = jnp.broadcast_to(packed[i:i + 1], packed.shape)
        chosen[i, :, 0, :] = same
        chosen[:, i, 1, :] = same

    my_block = col * n_row + row
    own_entries = pltpu.make_async_copy(chosen.at[row, home], entry_pairs.at[my_block], own_sem.at[3])
    own_entries.start()

    far = (2, 3, 1, 0)
    every = n_row * n_col

    def to_near(x, z, first, last):
        for k in range(first, last):
            y = far[k // 2]
            r = lax.bitwise_xor(row, x * 2 + y // 2)
            c = lax.bitwise_xor(col, z * 4 + y % 2 * 2 + 1 - k % 2)
            send(chosen.at[r, lax.div(c, n_col // n_row)], entry_pairs.at[my_block], PAIRS, r, c)

    def away(j):
        return jnp.where(j < 2, j + 2, 3 - j)

    lax.fori_loop(0, every // 8 - 1, lambda k, _: to_near(away(lax.div(k, 4)), away(lax.rem(k, 4)), 0, 8), None)
    to_near(0, 0, 0, 7)

    inverse = halves(panel_inv[...])
    wait_bytes(part_panel, recv_sem.at[PART_ROWS])
    part_factor[...] = dot_halves(halves(jnp.transpose(part_panel[...])), inverse)
    own_slab.wait()
    wait_bytes(slab_panel.at[pl.ds(0, (others + 1) * TILE)], recv_sem.at[SLAB_PASSED])
    tall = slab_factor.shape[0] // 4
    for step in range(4):
        rows = pl.ds(step * tall, tall)
        slab_factor[rows] = dot_halves(halves(jnp.transpose(slab_panel[:, rows])), inverse)
    wait_bytes(s_v.at[pl.ds(0, order - chunk)], send_sem.at[DUAL])
    wait_bytes(slab_panel.at[pl.ds(0, others * TILE)], send_sem.at[SLAB])
    wait_bytes(slab_panel.at[pl.ds(0, (others + 1) * TILE)], send_sem.at[SLAB_PASSED])
    wait_parts_sent(PART_ROWS, part_panel, part_panel.at[pl.ds(0, PW - TILE)])
    own_entries.wait()
    wait_bytes(entry_pairs.at[pl.ds(0, every - 1)], recv_sem.at[PAIRS])
    wait_bytes(entry_pairs.at[pl.ds(0, every - 1)], send_sem.at[PAIRS])


def finish_kernel(
    n_row, n_col,
    schur_prev, slab_factor, part_factor, entry_pairs, local_pos, panel_inv,
    updated, panel_factor,
    part_v, pairs_v, pos_v, inv_v, updated_v, factor_v, added, at_v, at_col_v, in_sem, out_sem,
):
    loads = [
        pltpu.make_async_copy(src, dst, in_sem.at[k])
        for k, (src, dst) in enumerate(
            (
                (local_pos, pos_v), (entry_pairs, pairs_v), (panel_inv, inv_v), (part_factor, part_v),
                (slab_factor, factor_v), (schur_prev, updated_v),
            )
        )
    ]
    for load in loads:
        load.start()
    row = lax.axis_index("row")
    col = lax.axis_index("col")
    slots, blocks = local_pos.shape
    per_row = slots // n_row
    slab = schur_prev.shape[0]
    steps = out_sem.shape[1]
    tall = slab // steps
    loads[0].wait()
    pos = pos_v[...]
    pos16 = pos.astype(BF16)

    def slot_lanes(slot):
        return jnp.sum(jnp.where(iota(pos.shape, 0) == slot, pos, 0.0), axis=0, keepdims=True) + PART // 2

    for step in range(steps):
        half = step * tall // PART
        within = (iota((tall, blocks), 0) + (step * tall - half * PART)).astype(F32)
        for u in range(2):
            hit = flag(within == slot_lanes(per_row * row + 2 * half + u))
            at_v[step, :, u * blocks:(u + 1) * blocks] = hit
            at_v[step, :, (2 + u) * blocks:(3 + u) * blocks] = hit
    across = iota((PART, blocks), 0).astype(F32)
    for u in range(2):
        hit = flag(across == slot_lanes(2 * col + u))
        at_col_v[:, u * blocks:(u + 1) * blocks] = hit
        at_col_v[:, (2 + u) * blocks:(3 + u) * blocks] = hit

    lanes = pairs_v.shape[1]
    in_tile, in_part = [], []
    for u in range(2):
        pick = flag(iota((slots, PW), 0) == 2 * (iota((slots, PW), 1) // TILE) + u)
        local = dot(pos16, pick, ((0,), (0,)))
        in_tile.append(local == (iota((blocks, PW), 1) % TILE - PART // 2).astype(F32))
        local = jnp.tile(dot(pos16, flag(iota((slots, lanes), 0) == 2 * col + u), ((0,), (0,))), (1, PART // lanes))
        in_part.append(local == (iota((blocks, PART), 1) - PART // 2).astype(F32))

    key = iota((lanes, PW), 0)
    tile = iota((lanes, PW), 1) // TILE
    own_key = iota((lanes, lanes), 0)

    def picked(entries, pick):
        both = dot(entries, pick)
        return both[:blocks] + both[blocks:]

    def panel_terms(entries, s4):
        terms = [jnp.where(in_tile[u], picked(entries, flag(key == s4 * slots + 2 * tile + u)), 0.0) for u in range(2)]
        return terms[0] + terms[1]

    def times_inverse(stacked):
        return halves(dot_halves(halves(stacked), inverse))

    loads[2].wait()
    inverse = halves(inv_v[...])
    loads[1].wait()
    own = jnp.concatenate(halves(pairs_v[pl.ds(0, blocks, stride=2), :]), axis=0)
    other = jnp.concatenate(halves(pairs_v[pl.ds(1, blocks, stride=2), :]), axis=0)
    first = 2 * lax.rem(col, n_col // n_row)
    terms = [panel_terms(other, first + u) for u in range(2)] + [panel_terms(own, s4) for s4 in range(per_row)]
    high, low = times_inverse(jnp.concatenate(terms, axis=0))
    deep = 2 * blocks
    loads[3].wait()
    factor = part_v[...] + dot(at_col_v[...], jnp.concatenate([high[:deep], low[:deep]], axis=0))
    columns = halves(factor)
    for half in range(2):
        mine = slice((half + 1) * deep, (half + 2) * deep)
        added[half, 0:deep, 0:PW] = high[mine]
        added[half, deep:, 0:PW] = low[mine]
        for u in range(2):
            s4 = 2 * half + u
            terms = [
                jnp.where(
                    in_part[v],
                    jnp.tile(picked(own, flag(own_key == s4 * slots + 2 * col + v)), (1, PART // lanes)),
                    0.0,
                )
                for v in range(2)
            ]
            up, down = halves(terms[0] + terms[1])
            added[half, u * blocks:(u + 1) * blocks, PW:] = up
            added[half, (2 + u) * blocks:(3 + u) * blocks, PW:] = down

    loads[4].wait()
    writes = []
    for step in range(steps):
        rows = pl.ds(step * tall, tall)
        sums = dot(at_v[step], added[step * tall // PART])
        factor = factor_v[rows] + sums[:, :PW]
        factor_v[rows] = factor
        writes.append(pltpu.make_async_copy(factor_v.at[rows], panel_factor.at[rows], out_sem.at[0, step]))
        writes[-1].start()
        if step == 0:
            loads[5].wait()
        updated_v[rows] = updated_v[rows] + sums[:, PW:] - dot_halves(halves(factor), columns, ((1,), (1,)))
        writes.append(pltpu.make_async_copy(updated_v.at[rows], updated.at[rows], out_sem.at[1, step]))
        writes[-1].start()
    for write in writes:
        write.wait()


def per_device(n_row, n_col, moment_x, moment_s, coeffs, slot_con, con_pos, schur_prev, panel_inv):
    count, order = coeffs.shape[1], coeffs.shape[2]
    blocks = slot_con.shape[0]
    slab, part = schur_prev.shape
    vmem = pl.BlockSpec(memory_space=pltpu.VMEM)
    hbm = pl.BlockSpec(memory_space=pltpu.HBM)
    lanes = (count // n_row) * count
    side = count * 8
    slab_factor, part_factor, entry_pairs, local_pos = pl.pallas_call(
        functools.partial(assemble_kernel, n_row, n_col),
        out_shape=(
            jax.ShapeDtypeStruct((slab, PW), F32),
            jax.ShapeDtypeStruct((part, PW), F32),
            jax.ShapeDtypeStruct((blocks, 2, lanes), F32),
            jax.ShapeDtypeStruct((count, blocks), F32),
        ),
        in_specs=[hbm, hbm, hbm, vmem, vmem, hbm, vmem],
        out_specs=(vmem, vmem, hbm, vmem),
        scratch_shapes=[
            pltpu.VMEM((PW, slab), F32),
            pltpu.VMEM((PW, part), F32),
            pltpu.VMEM((count, order, order), BF16),
            pltpu.VMEM((order // 16, count, 16, order), BF16),
            pltpu.VMEM((order, order), BF16),
            pltpu.VMEM((order, order), BF16),
            pltpu.VMEM((slab, 128), F32),
            pltpu.VMEM((TILE, slab), F32),
            pltpu.VMEM((side, side), F32),
            pltpu.VMEM((2, side, 2 * order), BF16),
            pltpu.VMEM((n_row, n_row, 2, lanes), F32),
            pltpu.SemaphoreType.DMA((4,)),
            pltpu.SemaphoreType.DMA((5,)),
            pltpu.SemaphoreType.DMA((6,)),
            pltpu.SemaphoreType.DMA((6,)),
            pltpu.SemaphoreType.REGULAR,
        ],
        compiler_params=pltpu.CompilerParams(
            collective_id=0, has_side_effects=True, vmem_limit_bytes=54 * 2**20
        ),
    )(moment_x, moment_s, coeffs, slot_con.T, con_pos.reshape(-1, 128), schur_prev, panel_inv)

    steps = 4
    return pl.pallas_call(
        functools.partial(finish_kernel, n_row, n_col),
        out_shape=(jax.ShapeDtypeStruct((slab, part), F32), jax.ShapeDtypeStruct((slab, PW), F32)),
        in_specs=[hbm] * 6,
        out_specs=(hbm, hbm),
        scratch_shapes=[
            pltpu.VMEM((part, PW), F32),
            pltpu.VMEM((2 * blocks, lanes), F32),
            pltpu.VMEM((count, blocks), F32),
            pltpu.VMEM((PW, PW), F32),
            pltpu.VMEM((slab, part), F32),
            pltpu.VMEM((slab, PW), F32),
            pltpu.VMEM((2, 4 * blocks, PW + part), BF16),
            pltpu.VMEM((steps, slab // steps, 4 * blocks), BF16),
            pltpu.VMEM((part, 4 * blocks), BF16),
            pltpu.SemaphoreType.DMA((6,)),
            pltpu.SemaphoreType.DMA((2, steps)),
        ],
        compiler_params=pltpu.CompilerParams(vmem_limit_bytes=63 * 2**20),
    )(schur_prev, slab_factor, part_factor, entry_pairs.reshape(2 * blocks, lanes), local_pos, panel_inv)


def solution(mesh):
    placed = (
        P("row", "col", None),
        P("row", "col", None),
        P(("row", "col"), None, None, None),
        P(),
        P(),
        P("row", "col"),
        P(),
    )
    return jax.shard_map(
        functools.partial(per_device, mesh.shape["row"], mesh.shape["col"]),
        mesh=mesh,
        in_specs=placed,
        out_specs=(P("row", "col"), P("row", None)),
        check_vma=False,
    )
```

```python
import functools

import jax
import jax.numpy as jnp
from jax import lax
from jax.experimental import pallas as pl
from jax.experimental.pallas import tpu as pltpu
from jax.sharding import PartitionSpec as P

TILE = 16
PW = 256
PART = 512
MESH = pl.DeviceIdType.MESH
F32 = jnp.float32
BF16 = jnp.bfloat16
PRIMAL, DUAL, SLAB, SLAB_PASSED, PART_ROWS, PAIRS = range(6)


def dot(a, b, dims=((1,), (0,)), precision=None):
    return lax.dot_general(a, b, (dims, ((), ())), precision=precision, preferred_element_type=F32)


def iota(shape, axis):
    return lax.broadcasted_iota(jnp.int32, shape, axis)


def halves(value):
    high = value.astype(BF16)
    return high, (value - high.astype(F32)).astype(BF16)


def dot_halves(a, b, dims=((1,), (0,))):
    a_high, a_low = a
    b_high, b_low = b
    return dot(a_high, b_high, dims) + dot(a_high, b_low, dims) + dot(a_low, b_high, dims)


def flag(condition):
    return jnp.where(condition, 1.0, 0.0).astype(BF16)


def assemble_kernel(
    n_row, n_col,
    moment_x, moment_s, coeffs, slot_con, con_pos, schur_prev, panel_inv,
    slab_factor, part_factor, entry_pairs, local_pos,
    slab_factor_v, part_factor_v, local_pos_v, slab_panel, part_panel, a_v, left_v, x_v, s_v, wide_v, own_panel, total, image_v, chosen,
    a_sem, own_sem, send_sem, recv_sem, everyone,
):
    row = lax.axis_index("row")
    col = lax.axis_index("col")
    count, order = a_v.shape[0], a_v.shape[1]
    chunk = order // n_col
    home = lax.div(col, n_col // n_row)

    a_parts = a_sem.shape[0]
    per_part = count // a_parts

    def a_copy(part):
        where = pl.ds(part * per_part, per_part)
        return pltpu.make_async_copy(coeffs.at[0, where], a_v.at[where], a_sem.at[part])

    my_chunk = pl.ds(pl.multiple_of(col * chunk, chunk), chunk)
    my_tile = pl.ds(pl.multiple_of(col * TILE, TILE), TILE)
    wide_copy = pltpu.make_async_copy(schur_prev.at[:, pl.ds(0, wide_v.shape[1])], wide_v, own_sem.at[4])
    own_x = pltpu.make_async_copy(moment_x.at[col], x_v.at[my_chunk], own_sem.at[PRIMAL])
    own_s = pltpu.make_async_copy(moment_s.at[col], s_v.at[my_chunk], own_sem.at[DUAL])
    wide_copy.start()
    own_x.start()
    own_s.start()
    lax.fori_loop(0, a_parts, lambda part, _: a_copy(part).start(), None)

    barrier = pltpu.get_barrier_semaphore()

    def greet(r, c):
        pl.semaphore_signal(barrier, inc=1, device_id=(r, c), device_id_type=MESH)

    lax.fori_loop(1, n_row, lambda k, _: greet(lax.rem(row + k, n_row), col), None)
    lax.fori_loop(1, n_col, lambda k, _: greet(row, lax.rem(col + k, n_col)), None)

    at_home = home == row
    pl.semaphore_wait(barrier, n_col - 1 + n_row - 1)

    def all_here(k, _):
        pl.semaphore_signal(everyone, inc=1, device_id=(lax.rem(row + k, n_row), col), device_id_type=MESH)

    def send(src, dst, which, r, c):
        pltpu.make_async_remote_copy(
            src_ref=src, dst_ref=dst, send_sem=send_sem.at[which], recv_sem=recv_sem.at[which],
            device_id=(r, c), device_id_type=MESH,
        ).start()

    def to_col(which, src, dst):
        def step(k, _):
            peer = lax.rem(col + k, n_col)
            send(src(peer), dst, which, row, peer)
        lax.fori_loop(1, n_col, step, None)

    halves_here = n_col // n_row

    def to_parts(which, src, dst):
        def step(k, _):
            r = lax.rem(row + k, n_row)
            for half in range(halves_here):
                c = row * halves_here + half

                @pl.when(jnp.logical_or(r != row, c != col))
                def _():
                    send(src(half), dst, which, r, c)

                @pl.when(jnp.logical_and(r == row, c == col))
                def _():
                    pltpu.make_async_copy(src(half), dst, recv_sem.at[which]).start()
        lax.fori_loop(0, n_row, step, None)

    def wait_bytes(ref, sem):
        pltpu.make_async_copy(ref, ref, sem).wait()

    def wait_parts_sent(which, whole, less):
        @pl.when(at_home)
        def _():
            wait_bytes(less, send_sem.at[which])

        @pl.when(jnp.logical_not(at_home))
        def _():
            wait_bytes(whole, send_sem.at[which])

    to_col(PRIMAL, lambda peer: moment_x.at[peer], x_v.at[my_chunk])
    lax.fori_loop(1, n_row, all_here, None)

    blocks = slot_con.shape[1]
    con = slot_con[...]
    perm = flag(iota((blocks, blocks), 1) == (iota((blocks, blocks), 0) % n_col) * n_row + iota((blocks, blocks), 0) // n_col)
    lanes = con_pos.shape[1]
    con_high = dot((con // lanes).astype(F32).astype(BF16), perm)
    con_low = dot((con % lanes).astype(F32).astype(BF16), perm)
    table = ((con_pos[...] % PART) - PART // 2).astype(F32).astype(BF16)
    high_iota = iota((con_pos.shape[0], blocks), 0).astype(F32)
    low_iota = iota((lanes, blocks), 0).astype(F32)
    for t in range(count):
        picked = dot(table, flag(high_iota == con_high[t:t + 1, :]), ((0,), (0,)))
        local_pos_v[t:t + 1, :] = jnp.sum(jnp.where(low_iota == con_low[t:t + 1, :], picked, 0.0), axis=0, keepdims=True)

    pos_out = pltpu.make_async_copy(local_pos_v, local_pos, own_sem.at[5])
    pos_out.start()
    wait_bytes(x_v.at[pl.ds(0, order - chunk)], send_sem.at[PRIMAL])
    to_col(DUAL, lambda peer: moment_s.at[peer], s_v.at[my_chunk])

    wide_copy.wait()
    own_panel[...] = jnp.transpose(wide_v[...])[:TILE, :]

    own_x.wait()
    wait_bytes(x_v.at[pl.ds(0, order - chunk)], recv_sem.at[PRIMAL])
    def lefts(part, _):
        a_copy(part).wait()
        for i in range(per_part):
            t = part * per_part + i
            left_v[:, t] = dot(x_v[...], a_v[t]).astype(BF16).reshape(groups, 16, order)

    groups = order // 16
    lax.fori_loop(0, a_parts // 2, lefts, None)
    pl.semaphore_wait(everyone, n_row - 1)

    sibling = lax.bitwise_xor(col, 1)
    others = n_col // 2 - 1
    own_slab = pltpu.make_async_copy(own_panel, slab_panel.at[my_tile], own_sem.at[SLAB])
    own_slab.start()
    send(own_panel, slab_panel.at[my_tile], SLAB_PASSED, row, sibling)

    def to_chip(k, _):
        send(own_panel, slab_panel.at[my_tile], SLAB, row, lax.rem(col + 2 * k, n_col))

    lax.fori_loop(1, n_col // 2, to_chip, None)
    to_parts(PART_ROWS, lambda half: own_panel.at[:, pl.ds(half * PART, PART)], part_panel.at[my_tile])

    lax.fori_loop(a_parts // 2, a_parts, lefts, None)

    own_s.wait()
    wait_bytes(s_v.at[pl.ds(0, order - chunk)], recv_sem.at[DUAL])
    side = total.shape[0]
    per_row = count // n_row
    total[...] = jnp.zeros_like(total)
    image_v[1] = jnp.zeros_like(image_v[1])

    def by_eights(value):
        value = value.reshape(count, 2, 8, order)
        return jnp.concatenate([value[:, h].reshape(side, order).astype(BF16) for h in range(2)], axis=1)

    def add_entries(g, slot):
        rows = pl.ds(pl.multiple_of(g * 16, 16), 16)
        coeff = a_v[:, rows, :].astype(F32).reshape(n_row, per_row, 16, order)
        coeff = jnp.transpose(coeff, (1, 0, 2, 3)).reshape(count, 16, order)
        total[...] += dot(by_eights(coeff), image_v[slot], ((1,), (1,)))

    unroll = 8

    def images(q, _):
        for i in range(unroll):
            g = q * unroll + i
            image = dot(left_v[g].reshape(count * 16, order), s_v[...])
            add_entries(jnp.maximum(g - 1, 0) if i == 0 else g - 1, (i + 1) % 2)
            image_v[i % 2] = by_eights(image)

    lax.fori_loop(0, groups // unroll * 3 // 4, images, None)

    wait_bytes(slab_panel.at[pl.ds(0, others * TILE)], recv_sem.at[SLAB])

    def pass_on(k, _):
        peer = lax.rem(col + 2 * k, n_col)
        tile = slab_panel.at[pl.ds(pl.multiple_of(peer * TILE, TILE), TILE)]
        send(tile, tile, SLAB_PASSED, row, sibling)

    lax.fori_loop(1, n_col // 2, pass_on, None)

    lax.fori_loop(groups // unroll * 3 // 4, groups // unroll, images, None)
    add_entries(groups - 1, 1)

    kept = jnp.where(iota((side, side), 0) % 8 == iota((side, side), 1) % 8, total[...], 0.0)
    by_slot = jnp.concatenate(halves(jnp.sum(kept.reshape(count, 8, side), axis=1)), axis=1)
    spread = dot(by_slot, flag(iota((2 * side, per_row * count), 1) % count == iota((2 * side, per_row * count), 0) % side // 8))
    packed = jnp.zeros((n_row, per_row * count), F32)
    for s4 in range(per_row):
        mine = spread[s4 * n_row:(s4 + 1) * n_row]
        packed += jnp.where(iota(mine.shape, 1) // count == s4, mine, 0.0)
    for i in range(n_row):
        same = jnp.broadcast_to(packed[i:i + 1], packed.shape)
        chosen[i, :, 0, :] = same
        chosen[:, i, 1, :] = same

    my_block = col * n_row + row
    own_entries = pltpu.make_async_copy(chosen.at[row, home], entry_pairs.at[my_block], own_sem.at[3])
    own_entries.start()

    far = (2, 3, 1, 0)
    every = n_row * n_col

    def to_near(x, z, first, last):
        for k in range(first, last):
            y = far[k // 2]
            r = lax.bitwise_xor(row, x * 2 + y // 2)
            c = lax.bitwise_xor(col, z * 4 + y % 2 * 2 + 1 - k % 2)
            send(chosen.at[r, lax.div(c, n_col // n_row)], entry_pairs.at[my_block], PAIRS, r, c)

    def away(j):
        return jnp.where(j < 2, j + 2, 3 - j)

    lax.fori_loop(0, every // 8 - 1, lambda k, _: to_near(away(lax.div(k, 4)), away(lax.rem(k, 4)), 0, 8), None)
    to_near(0, 0, 0, 7)

    inverse = halves(panel_inv[...])
    wait_bytes(part_panel, recv_sem.at[PART_ROWS])
    part_factor_v[...] = dot_halves(halves(jnp.transpose(part_panel[...])), inverse)
    part_out = pltpu.make_async_copy(part_factor_v, part_factor, own_sem.at[6])
    part_out.start()
    own_slab.wait()
    wait_bytes(slab_panel.at[pl.ds(0, (others + 1) * TILE)], recv_sem.at[SLAB_PASSED])
    tall = slab_factor.shape[0] // 4
    for step in range(4):
        rows = pl.ds(step * tall, tall)
        slab_factor_v[rows] = dot_halves(halves(jnp.transpose(slab_panel[:, rows])), inverse)
    slab_out = pltpu.make_async_copy(slab_factor_v, slab_factor, own_sem.at[7])
    slab_out.start()
    wait_bytes(s_v.at[pl.ds(0, order - chunk)], send_sem.at[DUAL])
    wait_bytes(slab_panel.at[pl.ds(0, others * TILE)], send_sem.at[SLAB])
    wait_bytes(slab_panel.at[pl.ds(0, (others + 1) * TILE)], send_sem.at[SLAB_PASSED])
    wait_parts_sent(PART_ROWS, part_panel, part_panel.at[pl.ds(0, PW - TILE)])
    own_entries.wait()
    pos_out.wait()
    part_out.wait()
    slab_out.wait()
    wait_bytes(entry_pairs.at[pl.ds(0, every - 1)], recv_sem.at[PAIRS])
    wait_bytes(entry_pairs.at[pl.ds(0, every - 1)], send_sem.at[PAIRS])


def finish_kernel(
    n_row, n_col,
    schur_prev, slab_factor, part_factor, entry_pairs, local_pos, panel_inv,
    updated, panel_factor,
    part_v, pairs_v, pos_v, inv_v, updated_v, factor_v, added, at_v, at_col_v, in_sem, out_sem,
):
    loads = [
        pltpu.make_async_copy(src, dst, in_sem.at[k])
        for k, (src, dst) in enumerate(
            (
                (local_pos, pos_v), (entry_pairs, pairs_v), (panel_inv, inv_v), (part_factor, part_v),
                (slab_factor, factor_v), (schur_prev, updated_v),
            )
        )
    ]
    for load in loads:
        load.start()
    row = lax.axis_index("row")
    col = lax.axis_index("col")
    slots, blocks = local_pos.shape
    per_row = slots // n_row
    slab = schur_prev.shape[0]
    steps = out_sem.shape[1]
    tall = slab // steps
    loads[0].wait()
    pos = pos_v[...]
    pos16 = pos.astype(BF16)

    def slot_lanes(slot):
        return jnp.sum(jnp.where(iota(pos.shape, 0) == slot, pos, 0.0), axis=0, keepdims=True) + PART // 2

    for step in range(steps):
        half = step * tall // PART
        within = (iota((tall, blocks), 0) + (step * tall - half * PART)).astype(F32)
        for u in range(2):
            hit = flag(within == slot_lanes(per_row * row + 2 * half + u))
            at_v[step, :, u * blocks:(u + 1) * blocks] = hit
            at_v[step, :, (2 + u) * blocks:(3 + u) * blocks] = hit
    across = iota((PART, blocks), 0).astype(F32)
    for u in range(2):
        hit = flag(across == slot_lanes(2 * col + u))
        at_col_v[:, u * blocks:(u + 1) * blocks] = hit
        at_col_v[:, (2 + u) * blocks:(3 + u) * blocks] = hit

    lanes = pairs_v.shape[1]
    in_tile, in_part = [], []
    for u in range(2):
        pick = flag(iota((slots, PW), 0) == 2 * (iota((slots, PW), 1) // TILE) + u)
        local = dot(pos16, pick, ((0,), (0,)))
        in_tile.append(local == (iota((blocks, PW), 1) % TILE - PART // 2).astype(F32))
        local = jnp.tile(dot(pos16, flag(iota((slots, lanes), 0) == 2 * col + u), ((0,), (0,))), (1, PART // lanes))
        in_part.append(local == (iota((blocks, PART), 1) - PART // 2).astype(F32))

    key = iota((lanes, PW), 0)
    tile = iota((lanes, PW), 1) // TILE
    own_key = iota((lanes, lanes), 0)

    def picked(entries, pick):
        both = dot(entries, pick)
        return both[:blocks] + both[blocks:]

    def panel_terms(entries, s4):
        terms = [jnp.where(in_tile[u], picked(entries, flag(key == s4 * slots + 2 * tile + u)), 0.0) for u in range(2)]
        return terms[0] + terms[1]

    def times_inverse(stacked):
        return halves(dot_halves(halves(stacked), inverse))

    loads[2].wait()
    inverse = halves(inv_v[...])
    loads[1].wait()
    own = jnp.concatenate(halves(pairs_v[pl.ds(0, blocks, stride=2), :]), axis=0)
    other = jnp.concatenate(halves(pairs_v[pl.ds(1, blocks, stride=2), :]), axis=0)
    first = 2 * lax.rem(col, n_col // n_row)
    terms = [panel_terms(other, first + u) for u in range(2)] + [panel_terms(own, s4) for s4 in range(per_row)]
    high, low = times_inverse(jnp.concatenate(terms, axis=0))
    deep = 2 * blocks
    loads[3].wait()
    factor = part_v[...] + dot(at_col_v[...], jnp.concatenate([high[:deep], low[:deep]], axis=0))
    columns = halves(factor)
    for half in range(2):
        mine = slice((half + 1) * deep, (half + 2) * deep)
        added[half, 0:deep, 0:PW] = high[mine]
        added[half, deep:, 0:PW] = low[mine]
        for u in range(2):
            s4 = 2 * half + u
            terms = [
                jnp.where(
                    in_part[v],
                    jnp.tile(picked(own, flag(own_key == s4 * slots + 2 * col + v)), (1, PART // lanes)),
                    0.0,
                )
                for v in range(2)
            ]
            up, down = halves(terms[0] + terms[1])
            added[half, u * blocks:(u + 1) * blocks, PW:] = up
            added[half, (2 + u) * blocks:(3 + u) * blocks, PW:] = down

    loads[4].wait()
    writes = []
    for step in range(steps):
        rows = pl.ds(step * tall, tall)
        sums = dot(at_v[step], added[step * tall // PART])
        factor = factor_v[rows] + sums[:, :PW]
        factor_v[rows] = factor
        writes.append(pltpu.make_async_copy(factor_v.at[rows], panel_factor.at[rows], out_sem.at[0, step]))
        writes[-1].start()
        if step == 0:
            loads[5].wait()
        updated_v[rows] = updated_v[rows] + sums[:, PW:] - dot_halves(halves(factor), columns, ((1,), (1,)))
        writes.append(pltpu.make_async_copy(updated_v.at[rows], updated.at[rows], out_sem.at[1, step]))
        writes[-1].start()
    for write in writes:
        write.wait()


def per_device(n_row, n_col, moment_x, moment_s, coeffs, slot_con, con_pos, schur_prev, panel_inv):
    count, order = coeffs.shape[1], coeffs.shape[2]
    blocks = slot_con.shape[0]
    slab, part = schur_prev.shape
    vmem = pl.BlockSpec(memory_space=pltpu.VMEM)
    hbm = pl.BlockSpec(memory_space=pltpu.HBM)
    lanes = (count // n_row) * count
    side = count * 8
    slab_factor, part_factor, entry_pairs, local_pos = pl.pallas_call(
        functools.partial(assemble_kernel, n_row, n_col),
        out_shape=(
            jax.ShapeDtypeStruct((slab, PW), F32),
            jax.ShapeDtypeStruct((part, PW), F32),
            jax.ShapeDtypeStruct((blocks, 2, lanes), F32),
            jax.ShapeDtypeStruct((count, blocks), F32),
        ),
        in_specs=[hbm, hbm, hbm, vmem, vmem, hbm, vmem],
        out_specs=(hbm, hbm, hbm, hbm),
        scratch_shapes=[
            pltpu.VMEM((slab, PW), F32),
            pltpu.VMEM((part, PW), F32),
            pltpu.VMEM((count, blocks), F32),
            pltpu.VMEM((PW, slab), F32),
            pltpu.VMEM((PW, part), F32),
            pltpu.VMEM((count, order, order), BF16),
            pltpu.VMEM((order // 16, count, 16, order), BF16),
            pltpu.VMEM((order, order), BF16),
            pltpu.VMEM((order, order), BF16),
            pltpu.VMEM((slab, 128), F32),
            pltpu.VMEM((TILE, slab), F32),
            pltpu.VMEM((side, side), F32),
            pltpu.VMEM((2, side, 2 * order), BF16),
            pltpu.VMEM((n_row, n_row, 2, lanes), F32),
            pltpu.SemaphoreType.DMA((4,)),
            pltpu.SemaphoreType.DMA((8,)),
            pltpu.SemaphoreType.DMA((6,)),
            pltpu.SemaphoreType.DMA((6,)),
            pltpu.SemaphoreType.REGULAR,
        ],
        compiler_params=pltpu.CompilerParams(
            collective_id=0, has_side_effects=True, vmem_limit_bytes=54 * 2**20
        ),
    )(moment_x, moment_s, coeffs, slot_con.T, con_pos.reshape(-1, 128), schur_prev, panel_inv)

    steps = 4
    return pl.pallas_call(
        functools.partial(finish_kernel, n_row, n_col),
        out_shape=(jax.ShapeDtypeStruct((slab, part), F32), jax.ShapeDtypeStruct((slab, PW), F32)),
        in_specs=[hbm] * 6,
        out_specs=(hbm, hbm),
        scratch_shapes=[
            pltpu.VMEM((part, PW), F32),
            pltpu.VMEM((2 * blocks, lanes), F32),
            pltpu.VMEM((count, blocks), F32),
            pltpu.VMEM((PW, PW), F32),
            pltpu.VMEM((slab, part), F32),
            pltpu.VMEM((slab, PW), F32),
            pltpu.VMEM((2, 4 * blocks, PW + part), BF16),
            pltpu.VMEM((steps, slab // steps, 4 * blocks), BF16),
            pltpu.VMEM((part, 4 * blocks), BF16),
            pltpu.SemaphoreType.DMA((6,)),
            pltpu.SemaphoreType.DMA((2, steps)),
        ],
        compiler_params=pltpu.CompilerParams(vmem_limit_bytes=63 * 2**20),
    )(schur_prev, slab_factor, part_factor, entry_pairs.reshape(2 * blocks, lanes), local_pos, panel_inv)


def solution(mesh):
    placed = (
        P("row", "col", None),
        P("row", "col", None),
        P(("row", "col"), None, None, None),
        P(),
        P(),
        P("row", "col"),
        P(),
    )
    return jax.shard_map(
        functools.partial(per_device, mesh.shape["row"], mesh.shape["col"]),
        mesh=mesh,
        in_specs=placed,
        out_specs=(P("row", "col"), P("row", None)),
        check_vma=False,
    )
```

```python
import functools

import jax
import jax.numpy as jnp
from jax import lax
from jax.experimental import pallas as pl
from jax.experimental.pallas import tpu as pltpu
from jax.sharding import PartitionSpec as P

TILE = 16
PW = 256
PART = 512
MESH = pl.DeviceIdType.MESH
F32 = jnp.float32
BF16 = jnp.bfloat16
PRIMAL, DUAL, SLAB, SLAB_PASSED, PART_ROWS, PAIRS = range(6)


def dot(a, b, dims=((1,), (0,)), precision=None):
    return lax.dot_general(a, b, (dims, ((), ())), precision=precision, preferred_element_type=F32)


def iota(shape, axis):
    return lax.broadcasted_iota(jnp.int32, shape, axis)


def halves(value):
    high = value.astype(BF16)
    return high, (value - high.astype(F32)).astype(BF16)


def dot_halves(a, b, dims=((1,), (0,))):
    a_high, a_low = a
    b_high, b_low = b
    return dot(a_high, b_high, dims) + dot(a_high, b_low, dims) + dot(a_low, b_high, dims)


def flag(condition):
    return jnp.where(condition, 1.0, 0.0).astype(BF16)


def assemble_kernel(
    n_row, n_col,
    moment_x, moment_s, coeffs, slot_con, con_pos, schur_prev, panel_inv,
    slab_factor, part_factor, entry_pairs, local_pos,
    slab_factor_v, part_factor_v, local_pos_v, slab_panel, part_panel, a_v, left_v, x_v, s_v, wide_v, own_panel, total, image_v, chosen,
    a_sem, own_sem, send_sem, recv_sem, everyone,
):
    row = lax.axis_index("row")
    col = lax.axis_index("col")
    count, order = a_v.shape[0], a_v.shape[1]
    chunk = order // n_col
    home = lax.div(col, n_col // n_row)

    a_parts = a_sem.shape[0]
    per_part = count // a_parts

    def a_copy(part):
        where = pl.ds(part * per_part, per_part)
        return pltpu.make_async_copy(coeffs.at[0, where], a_v.at[where], a_sem.at[part])

    my_chunk = pl.ds(pl.multiple_of(col * chunk, chunk), chunk)
    my_tile = pl.ds(pl.multiple_of(col * TILE, TILE), TILE)
    wide_copy = pltpu.make_async_copy(schur_prev.at[:, pl.ds(0, wide_v.shape[1])], wide_v, own_sem.at[4])
    own_x = pltpu.make_async_copy(moment_x.at[col], x_v.at[my_chunk], own_sem.at[PRIMAL])
    own_s = pltpu.make_async_copy(moment_s.at[col], s_v.at[my_chunk], own_sem.at[DUAL])
    wide_copy.start()
    own_x.start()
    own_s.start()
    lax.fori_loop(0, a_parts, lambda part, _: a_copy(part).start(), None)

    barrier = pltpu.get_barrier_semaphore()

    def greet(r, c):
        pl.semaphore_signal(barrier, inc=1, device_id=(r, c), device_id_type=MESH)

    lax.fori_loop(1, n_row, lambda k, _: greet(lax.rem(row + k, n_row), col), None)
    lax.fori_loop(1, n_col, lambda k, _: greet(row, lax.rem(col + k, n_col)), None)

    at_home = home == row
    pl.semaphore_wait(barrier, n_col - 1 + n_row - 1)

    def all_here(k, _):
        pl.semaphore_signal(everyone, inc=1, device_id=(lax.rem(row + k, n_row), col), device_id_type=MESH)

    def send(src, dst, which, r, c):
        pltpu.make_async_remote_copy(
            src_ref=src, dst_ref=dst, send_sem=send_sem.at[which], recv_sem=recv_sem.at[which],
            device_id=(r, c), device_id_type=MESH,
        ).start()

    def to_col(which, src, dst):
        def step(k, _):
            peer = lax.rem(col + k, n_col)
            send(src(peer), dst, which, row, peer)
        lax.fori_loop(1, n_col, step, None)

    halves_here = n_col // n_row

    def to_parts(which, src, dst):
        def step(k, _):
            r = lax.rem(row + k, n_row)
            for half in range(halves_here):
                c = row * halves_here + half

                @pl.when(jnp.logical_or(r != row, c != col))
                def _():
                    send(src(half), dst, which, r, c)

                @pl.when(jnp.logical_and(r == row, c == col))
                def _():
                    pltpu.make_async_copy(src(half), dst, recv_sem.at[which]).start()
        lax.fori_loop(0, n_row, step, None)

    def wait_bytes(ref, sem):
        pltpu.make_async_copy(ref, ref, sem).wait()

    def wait_parts_sent(which, whole, less):
        @pl.when(at_home)
        def _():
            wait_bytes(less, send_sem.at[which])

        @pl.when(jnp.logical_not(at_home))
        def _():
            wait_bytes(whole, send_sem.at[which])

    to_col(PRIMAL, lambda peer: moment_x.at[peer], x_v.at[my_chunk])
    lax.fori_loop(1, n_row, all_here, None)

    blocks = slot_con.shape[1]
    con = slot_con[...]
    perm = flag(iota((blocks, blocks), 1) == (iota((blocks, blocks), 0) % n_col) * n_row + iota((blocks, blocks), 0) // n_col)
    lanes = con_pos.shape[1]
    con_high = dot((con // lanes).astype(F32).astype(BF16), perm)
    con_low = dot((con % lanes).astype(F32).astype(BF16), perm)
    table = ((con_pos[...] % PART) - PART // 2).astype(F32).astype(BF16)
    high_iota = iota((con_pos.shape[0], blocks), 0).astype(F32)
    low_iota = iota((lanes, blocks), 0).astype(F32)
    for t in range(count):
        picked = dot(table, flag(high_iota == con_high[t:t + 1, :]), ((0,), (0,)))
        local_pos_v[t:t + 1, :] = jnp.sum(jnp.where(low_iota == con_low[t:t + 1, :], picked, 0.0), axis=0, keepdims=True)

    pos_out = pltpu.make_async_copy(local_pos_v, local_pos, own_sem.at[5])
    pos_out.start()
    wait_bytes(x_v.at[pl.ds(0, order - chunk)], send_sem.at[PRIMAL])
    to_col(DUAL, lambda peer: moment_s.at[peer], s_v.at[my_chunk])

    wide_copy.wait()
    own_panel[...] = jnp.transpose(wide_v[...])[:TILE, :]

    own_x.wait()
    wait_bytes(x_v.at[pl.ds(0, order - chunk)], recv_sem.at[PRIMAL])
    def lefts(part, _):
        a_copy(part).wait()
        for i in range(per_part):
            t = part * per_part + i
            left_v[:, t] = dot(x_v[...], a_v[t]).astype(BF16).reshape(groups, 16, order)

    groups = order // 16
    lax.fori_loop(0, a_parts // 2, lefts, None)
    pl.semaphore_wait(everyone, n_row - 1)

    sibling = lax.bitwise_xor(col, 1)
    others = n_col // 2 - 1
    own_slab = pltpu.make_async_copy(own_panel, slab_panel.at[my_tile], own_sem.at[SLAB])
    own_slab.start()
    send(own_panel, slab_panel.at[my_tile], SLAB_PASSED, row, sibling)

    def to_chip(k, _):
        send(own_panel, slab_panel.at[my_tile], SLAB, row, lax.rem(col + 2 * k, n_col))

    lax.fori_loop(1, n_col // 2, to_chip, None)

    lax.fori_loop(a_parts // 2, a_parts - 1, lefts, None)
    to_parts(PART_ROWS, lambda half: own_panel.at[:, pl.ds(half * PART, PART)], part_panel.at[my_tile])
    lax.fori_loop(a_parts - 1, a_parts, lefts, None)

    own_s.wait()
    wait_bytes(s_v.at[pl.ds(0, order - chunk)], recv_sem.at[DUAL])
    side = total.shape[0]
    per_row = count // n_row
    total[...] = jnp.zeros_like(total)
    image_v[1] = jnp.zeros_like(image_v[1])

    def by_eights(value):
        value = value.reshape(count, 2, 8, order)
        return jnp.concatenate([value[:, h].reshape(side, order).astype(BF16) for h in range(2)], axis=1)

    def add_entries(g, slot):
        rows = pl.ds(pl.multiple_of(g * 16, 16), 16)
        coeff = a_v[:, rows, :].astype(F32).reshape(n_row, per_row, 16, order)
        coeff = jnp.transpose(coeff, (1, 0, 2, 3)).reshape(count, 16, order)
        total[...] += dot(by_eights(coeff), image_v[slot], ((1,), (1,)))

    unroll = 8

    def images(q, _):
        for i in range(unroll):
            g = q * unroll + i
            image = dot(left_v[g].reshape(count * 16, order), s_v[...])
            add_entries(jnp.maximum(g - 1, 0) if i == 0 else g - 1, (i + 1) % 2)
            image_v[i % 2] = by_eights(image)

    lax.fori_loop(0, groups // unroll * 3 // 4, images, None)

    wait_bytes(slab_panel.at[pl.ds(0, others * TILE)], recv_sem.at[SLAB])

    def pass_on(k, _):
        peer = lax.rem(col + 2 * k, n_col)
        tile = slab_panel.at[pl.ds(pl.multiple_of(peer * TILE, TILE), TILE)]
        send(tile, tile, SLAB_PASSED, row, sibling)

    lax.fori_loop(1, n_col // 2, pass_on, None)

    lax.fori_loop(groups // unroll * 3 // 4, groups // unroll, images, None)
    add_entries(groups - 1, 1)

    kept = jnp.where(iota((side, side), 0) % 8 == iota((side, side), 1) % 8, total[...], 0.0)
    by_slot = jnp.concatenate(halves(jnp.sum(kept.reshape(count, 8, side), axis=1)), axis=1)
    spread = dot(by_slot, flag(iota((2 * side, per_row * count), 1) % count == iota((2 * side, per_row * count), 0) % side // 8))
    packed = jnp.zeros((n_row, per_row * count), F32)
    for s4 in range(per_row):
        mine = spread[s4 * n_row:(s4 + 1) * n_row]
        packed += jnp.where(iota(mine.shape, 1) // count == s4, mine, 0.0)
    for i in range(n_row):
        same = jnp.broadcast_to(packed[i:i + 1], packed.shape)
        chosen[i, :, 0, :] = same
        chosen[:, i, 1, :] = same

    my_block = col * n_row + row
    own_entries = pltpu.make_async_copy(chosen.at[row, home], entry_pairs.at[my_block], own_sem.at[3])
    own_entries.start()

    far = (2, 3, 1, 0)
    every = n_row * n_col

    def to_near(x, z, first, last):
        for k in range(first, last):
            y = far[k // 2]
            r = lax.bitwise_xor(row, x * 2 + y // 2)
            c = lax.bitwise_xor(col, z * 4 + y % 2 * 2 + 1 - k % 2)
            send(chosen.at[r, lax.div(c, n_col // n_row)], entry_pairs.at[my_block], PAIRS, r, c)

    def away(j):
        return jnp.where(j < 2, j + 2, 3 - j)

    lax.fori_loop(0, every // 8 - 1, lambda k, _: to_near(away(lax.div(k, 4)), away(lax.rem(k, 4)), 0, 8), None)
    to_near(0, 0, 0, 7)

    inverse = halves(panel_inv[...])
    wait_bytes(part_panel, recv_sem.at[PART_ROWS])
    part_factor_v[...] = dot_halves(halves(jnp.transpose(part_panel[...])), inverse)
    part_out = pltpu.make_async_copy(part_factor_v, part_factor, own_sem.at[6])
    part_out.start()
    own_slab.wait()
    wait_bytes(slab_panel.at[pl.ds(0, (others + 1) * TILE)], recv_sem.at[SLAB_PASSED])
    tall = slab_factor.shape[0] // 4
    for step in range(4):
        rows = pl.ds(step * tall, tall)
        slab_factor_v[rows] = dot_halves(halves(jnp.transpose(slab_panel[:, rows])), inverse)
    slab_out = pltpu.make_async_copy(slab_factor_v, slab_factor, own_sem.at[7])
    slab_out.start()
    wait_bytes(s_v.at[pl.ds(0, order - chunk)], send_sem.at[DUAL])
    wait_bytes(slab_panel.at[pl.ds(0, others * TILE)], send_sem.at[SLAB])
    wait_bytes(slab_panel.at[pl.ds(0, (others + 1) * TILE)], send_sem.at[SLAB_PASSED])
    wait_parts_sent(PART_ROWS, part_panel, part_panel.at[pl.ds(0, PW - TILE)])
    own_entries.wait()
    pos_out.wait()
    part_out.wait()
    slab_out.wait()
    wait_bytes(entry_pairs.at[pl.ds(0, every - 1)], recv_sem.at[PAIRS])
    wait_bytes(entry_pairs.at[pl.ds(0, every - 1)], send_sem.at[PAIRS])


def finish_kernel(
    n_row, n_col,
    schur_prev, slab_factor, part_factor, entry_pairs, local_pos, panel_inv,
    updated, panel_factor,
    part_v, pairs_v, pos_v, inv_v, updated_v, factor_v, added, at_v, at_col_v, in_sem, out_sem,
):
    loads = [
        pltpu.make_async_copy(src, dst, in_sem.at[k])
        for k, (src, dst) in enumerate(
            (
                (local_pos, pos_v), (entry_pairs, pairs_v), (panel_inv, inv_v), (part_factor, part_v),
                (slab_factor, factor_v), (schur_prev, updated_v),
            )
        )
    ]
    for load in loads:
        load.start()
    row = lax.axis_index("row")
    col = lax.axis_index("col")
    slots, blocks = local_pos.shape
    per_row = slots // n_row
    slab = schur_prev.shape[0]
    steps = out_sem.shape[1]
    tall = slab // steps
    loads[0].wait()
    pos = pos_v[...]
    pos16 = pos.astype(BF16)

    def slot_lanes(slot):
        return jnp.sum(jnp.where(iota(pos.shape, 0) == slot, pos, 0.0), axis=0, keepdims=True) + PART // 2

    for step in range(steps):
        half = step * tall // PART
        within = (iota((tall, blocks), 0) + (step * tall - half * PART)).astype(F32)
        for u in range(2):
            hit = flag(within == slot_lanes(per_row * row + 2 * half + u))
            at_v[step, :, u * blocks:(u + 1) * blocks] = hit
            at_v[step, :, (2 + u) * blocks:(3 + u) * blocks] = hit
    across = iota((PART, blocks), 0).astype(F32)
    for u in range(2):
        hit = flag(across == slot_lanes(2 * col + u))
        at_col_v[:, u * blocks:(u + 1) * blocks] = hit
        at_col_v[:, (2 + u) * blocks:(3 + u) * blocks] = hit

    lanes = pairs_v.shape[1]
    in_tile, in_part = [], []
    for u in range(2):
        pick = flag(iota((slots, PW), 0) == 2 * (iota((slots, PW), 1) // TILE) + u)
        local = dot(pos16, pick, ((0,), (0,)))
        in_tile.append(local == (iota((blocks, PW), 1) % TILE - PART // 2).astype(F32))
        local = jnp.tile(dot(pos16, flag(iota((slots, lanes), 0) == 2 * col + u), ((0,), (0,))), (1, PART // lanes))
        in_part.append(local == (iota((blocks, PART), 1) - PART // 2).astype(F32))

    key = iota((lanes, PW), 0)
    tile = iota((lanes, PW), 1) // TILE
    own_key = iota((lanes, lanes), 0)

    def picked(entries, pick):
        both = dot(entries, pick)
        return both[:blocks] + both[blocks:]

    def panel_terms(entries, s4):
        terms = [jnp.where(in_tile[u], picked(entries, flag(key == s4 * slots + 2 * tile + u)), 0.0) for u in range(2)]
        return terms[0] + terms[1]

    def times_inverse(stacked):
        return halves(dot_halves(halves(stacked), inverse))

    loads[2].wait()
    inverse = halves(inv_v[...])
    loads[1].wait()
    own = jnp.concatenate(halves(pairs_v[pl.ds(0, blocks, stride=2), :]), axis=0)
    other = jnp.concatenate(halves(pairs_v[pl.ds(1, blocks, stride=2), :]), axis=0)
    first = 2 * lax.rem(col, n_col // n_row)
    terms = [panel_terms(other, first + u) for u in range(2)] + [panel_terms(own, s4) for s4 in range(per_row)]
    high, low = times_inverse(jnp.concatenate(terms, axis=0))
    deep = 2 * blocks
    loads[3].wait()
    factor = part_v[...] + dot(at_col_v[...], jnp.concatenate([high[:deep], low[:deep]], axis=0))
    columns = halves(factor)
    for half in range(2):
        mine = slice((half + 1) * deep, (half + 2) * deep)
        added[half, 0:deep, 0:PW] = high[mine]
        added[half, deep:, 0:PW] = low[mine]
        for u in range(2):
            s4 = 2 * half + u
            terms = [
                jnp.where(
                    in_part[v],
                    jnp.tile(picked(own, flag(own_key == s4 * slots + 2 * col + v)), (1, PART // lanes)),
                    0.0,
                )
                for v in range(2)
            ]
            up, down = halves(terms[0] + terms[1])
            added[half, u * blocks:(u + 1) * blocks, PW:] = up
            added[half, (2 + u) * blocks:(3 + u) * blocks, PW:] = down

    loads[4].wait()
    writes = []
    for step in range(steps):
        rows = pl.ds(step * tall, tall)
        sums = dot(at_v[step], added[step * tall // PART])
        factor = factor_v[rows] + sums[:, :PW]
        factor_v[rows] = factor
        writes.append(pltpu.make_async_copy(factor_v.at[rows], panel_factor.at[rows], out_sem.at[0, step]))
        writes[-1].start()
        if step == 0:
            loads[5].wait()
        updated_v[rows] = updated_v[rows] + sums[:, PW:] - dot_halves(halves(factor), columns, ((1,), (1,)))
        writes.append(pltpu.make_async_copy(updated_v.at[rows], updated.at[rows], out_sem.at[1, step]))
        writes[-1].start()
    for write in writes:
        write.wait()


def per_device(n_row, n_col, moment_x, moment_s, coeffs, slot_con, con_pos, schur_prev, panel_inv):
    count, order = coeffs.shape[1], coeffs.shape[2]
    blocks = slot_con.shape[0]
    slab, part = schur_prev.shape
    vmem = pl.BlockSpec(memory_space=pltpu.VMEM)
    hbm = pl.BlockSpec(memory_space=pltpu.HBM)
    lanes = (count // n_row) * count
    side = count * 8
    slab_factor, part_factor, entry_pairs, local_pos = pl.pallas_call(
        functools.partial(assemble_kernel, n_row, n_col),
        out_shape=(
            jax.ShapeDtypeStruct((slab, PW), F32),
            jax.ShapeDtypeStruct((part, PW), F32),
            jax.ShapeDtypeStruct((blocks, 2, lanes), F32),
            jax.ShapeDtypeStruct((count, blocks), F32),
        ),
        in_specs=[hbm, hbm, hbm, vmem, vmem, hbm, vmem],
        out_specs=(hbm, hbm, hbm, hbm),
        scratch_shapes=[
            pltpu.VMEM((slab, PW), F32),
            pltpu.VMEM((part, PW), F32),
            pltpu.VMEM((count, blocks), F32),
            pltpu.VMEM((PW, slab), F32),
            pltpu.VMEM((PW, part), F32),
            pltpu.VMEM((count, order, order), BF16),
            pltpu.VMEM((order // 16, count, 16, order), BF16),
            pltpu.VMEM((order, order), BF16),
            pltpu.VMEM((order, order), BF16),
            pltpu.VMEM((slab, 128), F32),
            pltpu.VMEM((TILE, slab), F32),
            pltpu.VMEM((side, side), F32),
            pltpu.VMEM((2, side, 2 * order), BF16),
            pltpu.VMEM((n_row, n_row, 2, lanes), F32),
            pltpu.SemaphoreType.DMA((4,)),
            pltpu.SemaphoreType.DMA((8,)),
            pltpu.SemaphoreType.DMA((6,)),
            pltpu.SemaphoreType.DMA((6,)),
            pltpu.SemaphoreType.REGULAR,
        ],
        compiler_params=pltpu.CompilerParams(
            collective_id=0, has_side_effects=True, vmem_limit_bytes=54 * 2**20
        ),
    )(moment_x, moment_s, coeffs, slot_con.T, con_pos.reshape(-1, 128), schur_prev, panel_inv)

    steps = 4
    return pl.pallas_call(
        functools.partial(finish_kernel, n_row, n_col),
        out_shape=(jax.ShapeDtypeStruct((slab, part), F32), jax.ShapeDtypeStruct((slab, PW), F32)),
        in_specs=[hbm] * 6,
        out_specs=(hbm, hbm),
        scratch_shapes=[
            pltpu.VMEM((part, PW), F32),
            pltpu.VMEM((2 * blocks, lanes), F32),
            pltpu.VMEM((count, blocks), F32),
            pltpu.VMEM((PW, PW), F32),
            pltpu.VMEM((slab, part), F32),
            pltpu.VMEM((slab, PW), F32),
            pltpu.VMEM((2, 4 * blocks, PW + part), BF16),
            pltpu.VMEM((steps, slab // steps, 4 * blocks), BF16),
            pltpu.VMEM((part, 4 * blocks), BF16),
            pltpu.SemaphoreType.DMA((6,)),
            pltpu.SemaphoreType.DMA((2, steps)),
        ],
        compiler_params=pltpu.CompilerParams(vmem_limit_bytes=63 * 2**20),
    )(schur_prev, slab_factor, part_factor, entry_pairs.reshape(2 * blocks, lanes), local_pos, panel_inv)


def solution(mesh):
    placed = (
        P("row", "col", None),
        P("row", "col", None),
        P(("row", "col"), None, None, None),
        P(),
        P(),
        P("row", "col"),
        P(),
    )
    return jax.shard_map(
        functools.partial(per_device, mesh.shape["row"], mesh.shape["col"]),
        mesh=mesh,
        in_specs=placed,
        out_specs=(P("row", "col"), P("row", None)),
        check_vma=False,
    )
```
